128 devices in a mesh: ctx: 8 (over x, z_lo), rows: 16 (over z_hi, y, core).
Axes of the slice: x: 4, y: 4, z: 4 (z_hi: 2, z_lo: 2; z = z_hi * 2 + z_lo), core: 2. Of those that a mesh axis runs over, the one named last changes fastest.
Arguments:
- queries: bfloat16 [16384, 4096], P('ctx', 'rows'), as said below
- keys: bfloat16 [16384, 1024], P('ctx'), as said below
- values: bfloat16 [16384, 1024], P('ctx'), may hold values from -6 to 6
- verticals: int32 [32, 8], P('rows'), may hold values from 0 to 127
- slashes: int32 [32, 16], P('rows'), may hold values from 1 to 127
- destination: int32 [16384], P('ctx'), may hold values from 0 to 16383, as said below
Outputs:
- remapped: bfloat16 [16384, 4096], P(('ctx', 'rows'))
The draws below stay inside these ranges and needn't reach their ends.
Inputs may be any that keep to these rules, and one draw needn't show every extreme that they name: queries lie within -9 to 9. keys lie within -4 to 4. destination is a permutation of the 16384 rows; within each aligned block of 128 output rows the tokens stand in ascending order; of the 2048 tokens of one aligned token shard at most 32 go to one such block, and in every draw some shard sends exactly 32 to some block.
All inputs are finite; a program needn't handle non-finite values.
Results may differ from the reference program's by a relative error of at most 0.018.
Values may be sent and summed in bfloat16 or wider, within the bound.
No kernel may reach another device: no remote copies, remote signals or barrier semaphores. Data moves between devices by JAX's collectives and lax.ppermute only.
A program may use at most 320 MiB of HBM per device.

```python
import jax
import jax.numpy as jnp
from jax import lax

HEADS = 32
KV_HEADS = 8
DH = 128
BLOCK = 128
NV = 8
NSL = 16
TOK_DEV = 2048
TOKENS = 16384
NBLOCKS = 128
N_CTX = 8
N_ROWS = 16


def common_keys(key):
    shape = (TOKENS, KV_HEADS * DH)
    base = jnp.clip(jax.random.normal(key, shape, jnp.float32), -4.0, 4.0)
    rows = jnp.arange(TOKENS, dtype=jnp.int32)
    within = rows % BLOCK
    chosen = rows // BLOCK % 4 == 1
    first_row = (chosen & (within == 2))[:, None]
    second_row = (chosen & (within == 3))[:, None]
    result = jnp.where(first_row, base, base)
    result = jnp.where(second_row, base, result)
    return result


def draw_keys(key, part):
    result = common_keys(key)
    return result.astype(jnp.bfloat16)


def draw_queries(key, part):
    key = jax.random.fold_in(key, 5)
    return jnp.clip(jax.random.normal(key, (TOKENS, HEADS * DH), jnp.float32), -4.0, 4.0).astype(jnp.bfloat16)


def draw_destination(key, part):
    key = jax.random.fold_in(key, 7)
    share = TOK_DEV // (N_CTX * N_ROWS)
    half = N_CTX // 2
    owners = N_CTX * N_ROWS
    swing = jax.random.randint(jax.random.fold_in(key, 1), (N_ROWS, half), -share, share + 1, jnp.int32)
    swing = swing.at[:, 0].set(share)
    loads = jnp.concatenate([share + swing, share - swing], axis=1)
    sort_orders = jax.vmap(lambda single: jax.random.permutation(single, N_CTX))(jax.random.split(jax.random.fold_in(key, 2), N_ROWS))
    loads = jnp.take_along_axis(loads, sort_orders.astype(jnp.int32), axis=1)
    shard = jnp.arange(N_CTX, dtype=jnp.int32)
    lag = (shard[None, :] - shard[:, None]) % N_CTX
    counts = jnp.transpose(loads[:, lag], (1, 2, 0)).reshape(N_CTX, owners)
    bounds = jnp.cumsum(counts, axis=1).astype(jnp.int32)
    shuffles = jax.vmap(lambda single: jax.random.permutation(single, TOK_DEV))(jax.random.split(jax.random.fold_in(key, 3), N_CTX)).astype(jnp.int32)
    places = jnp.arange(TOK_DEV, dtype=jnp.int32)
    owner_at = jnp.sum((places[None, :, None] >= bounds[:, None, :]).astype(jnp.int32), axis=2)
    shard_index = jnp.broadcast_to(shard[:, None], (N_CTX, TOK_DEV))
    owner_token = jnp.zeros((N_CTX, TOK_DEV), jnp.int32).at[shard_index, shuffles].set(owner_at)
    owner_flat = owner_token.reshape(TOKENS)
    order = jnp.argsort(owner_flat, stable=True).astype(jnp.int32)
    return jnp.zeros((TOKENS,), jnp.int32).at[order].set(jnp.arange(TOKENS, dtype=jnp.int32))


def place_ends(array, own_key, low, top_value):
    longest = array.shape.index(max(array.shape))
    spots = []
    for shift in (0, 1):
        where = [jax.random.randint(jax.random.fold_in(own_key, axis), (), 0, length) for axis, length in enumerate(array.shape)]
        where[longest] = (where[longest] + shift) % array.shape[longest]
        spots.append(tuple(where))
    return array.at[spots[0]].set(low).at[spots[1]].set(top_value)


def block_scale(rng, dims, cuts, low, high):
    def one(dim, blocks):
        steps = jax.random.uniform(jax.random.fold_in(jax.random.fold_in(rng, 6), dim), (blocks,), jnp.float32, low / len(cuts), high / len(cuts))
        return jnp.repeat(jnp.exp(steps), dims[dim] // blocks).reshape((-1,) + (1,) * (len(dims) - dim - 1))

    factor_of = one(*cuts[0])
    for cut in cuts[1:]:
        factor_of = factor_of * one(*cut)
    return factor_of


def bell_draw(key, dims, deviation, bound, cuts=(), held_as=jnp.bfloat16):
    level = block_scale(key, dims, cuts, -0.22, 0.18) if cuts else 1.0
    drawn = jax.random.normal(key, dims, jnp.float32) * deviation * level
    return jnp.minimum(jnp.maximum(drawn, -bound), bound).astype(held_as)


def setup_inputs(seed: int = 0) -> dict:
    splits = jax.random.split(jax.random.key(seed), 7)
    queries = draw_queries(jax.random.fold_in(splits[6], 71), 0)
    keys = draw_keys(jax.random.fold_in(splits[6], 71), 0)
    values = bell_draw(splits[2], (TOKENS, KV_HEADS * DH), 1.0, 6.0, ((0, 8),))
    verticals = place_ends(jax.random.randint(splits[3], (HEADS, NV), 0, NBLOCKS), jax.random.fold_in(splits[3], 1), 0, NBLOCKS - 1).astype(jnp.int32)
    slashes = place_ends(jax.random.randint(splits[4], (HEADS, NSL), 1, NBLOCKS), jax.random.fold_in(splits[4], 1), 1, NBLOCKS - 1).astype(jnp.int32)
    destination = draw_destination(jax.random.fold_in(splits[6], 71), 0)
    return {"queries": queries, "keys": keys, "values": values, "verticals": verticals, "slashes": slashes, "destination": destination}


NEG = -1e30


def reference(queries, keys, values, verticals, slashes, destination):
    share = HEADS // KV_HEADS
    scale = DH ** -0.5
    query_heads = queries.reshape(TOKENS, HEADS, DH)
    key_heads = keys.reshape(TOKENS, KV_HEADS, DH)
    value_heads = values.reshape(TOKENS, KV_HEADS, DH)
    key_pos = jnp.arange(TOKENS, dtype=jnp.int32)
    all_blocks = jnp.arange(NBLOCKS, dtype=jnp.int32)

    def one_head(head):
        query_rows = lax.dynamic_index_in_dim(query_heads, head, 1, keepdims=False)
        kv_index = head // share
        key_rows = lax.dynamic_index_in_dim(key_heads, kv_index, 1, keepdims=False)
        value_rows = lax.dynamic_index_in_dim(value_heads, kv_index, 1, keepdims=False)
        vertical = lax.dynamic_index_in_dim(verticals, head, 0, keepdims=False)
        slash = lax.dynamic_index_in_dim(slashes, head, 0, keepdims=False)
        vertical_hit = jnp.any(vertical[:, None] == all_blocks[None, :], axis=0)

        def one_block(start):
            query_block = lax.dynamic_slice_in_dim(query_rows, start, TOK_DEV, 0)
            query_pos = start + jnp.arange(TOK_DEV, dtype=jnp.int32)
            query_blocks = start // BLOCK + jnp.arange(TOK_DEV // BLOCK, dtype=jnp.int32)
            offset = query_blocks[:, None] - all_blocks[None, :]
            slash_hit = jnp.any(slash[:, None, None] == offset[None, :, :], axis=0)
            block_hit = (offset == 0) | vertical_hit[None, :] | slash_hit
            token_hit = jnp.repeat(jnp.repeat(block_hit, BLOCK, axis=0), BLOCK, axis=1)
            allowed = token_hit & (key_pos[None, :] <= query_pos[:, None])
            scores = jnp.dot(query_block, key_rows.T, preferred_element_type=jnp.float32) * scale
            row_max = jnp.max(jnp.where(allowed, scores, NEG), axis=1)
            weights = jnp.where(allowed, jnp.exp(scores - row_max[:, None]), 0.0)
            total = jnp.sum(weights, axis=1)
            mixed = jnp.dot(weights.astype(jnp.bfloat16), value_rows, preferred_element_type=jnp.float32)
            return (mixed / total[:, None]).astype(jnp.bfloat16)

        starts = jnp.arange(N_CTX, dtype=jnp.int32) * TOK_DEV
        return lax.map(one_block, starts).reshape(TOKENS, DH)

    per_head = lax.map(one_head, jnp.arange(HEADS, dtype=jnp.int32))
    attended = jnp.transpose(per_head, (1, 0, 2)).reshape(TOKENS, HEADS * DH)
    remapped = jnp.zeros((TOKENS, HEADS * DH), jnp.bfloat16).at[destination].set(attended)
    return remapped
```

```python
import functools

import jax
import jax.numpy as jnp
from jax import lax
from jax.experimental import pallas as pl
from jax.experimental.pallas import tpu as pltpu
from jax.sharding import PartitionSpec as P

HEADS = 32
KV_HEADS = 8
DH = 128
BLOCK = 128
NEG = -1e30
ROW_CEILING = 1 << 30
EMPTY = 1048576.0
SCALE2 = DH**-0.5 * 1.4426950408889634
GROUP = 4
PIECE = {(0, 0): 0, (3, 0): 1, (1, 0): 2, (0, 1): 3, (2, 0): 4, (1, 1): 5, (3, 1): 6, (2, 1): 7}
ANY = pl.BlockSpec(memory_space=pl.ANY)
SMEM = pl.BlockSpec(memory_space=pltpu.SMEM)
VMEM = pl.BlockSpec(memory_space=pltpu.VMEM)


def dot_t(a, b):
    return lax.dot_general(a, b, (((1,), (1,)), ((), ())), preferred_element_type=jnp.float32)


def attend_kernel(pieces, slots, heads, meta, lists, counts, first_row, sent, q_ref, dest_ref, keys, values, *rest):
    mine, other = rest[: pieces - 1], rest[pieces - 1 : 2 * pieces - 2]
    out_ref, k_s, v_s, att, sem = rest[2 * pieces - 2 :]
    shard = q_ref.shape[0]
    nblk = shard // BLOCK
    core, kv = meta[0], meta[1]
    column = pl.ds(pl.multiple_of(kv * DH, DH), DH)

    def spot(ref, p):
        return ref.at[pl.ds(p * shard, shard)]

    pltpu.make_async_copy(keys.at[:, column], spot(k_s, 0), sem.at[0]).start()
    pltpu.make_async_copy(values.at[:, column], spot(v_s, 0), sem.at[pieces]).start()
    for p in range(1, pieces):

        @pl.when(core == 0)
        def _():
            pltpu.make_async_copy(mine[p - 1], spot(k_s, p), sem.at[p]).start()
            pltpu.make_async_copy(other[p - 1], spot(v_s, p), sem.at[pieces + p]).start()

        @pl.when(core != 0)
        def _():
            pltpu.make_async_copy(other[p - 1], spot(k_s, p), sem.at[p]).start()
            pltpu.make_async_copy(mine[p - 1], spot(v_s, p), sem.at[pieces + p]).start()

    pltpu.make_async_copy(keys.at[:, column], spot(k_s, 0), sem.at[0]).wait()
    pltpu.make_async_copy(values.at[:, column], spot(v_s, 0), sem.at[pieces]).wait()
    for p in range(1, pieces):
        pltpu.make_async_copy(mine[p - 1], spot(k_s, p), sem.at[p]).wait()
        pltpu.make_async_copy(mine[p - 1], spot(v_s, p), sem.at[pieces + p]).wait()

    def block_of(ref, index):
        return ref[pl.ds(pl.multiple_of(index * BLOCK, BLOCK), BLOCK), :]

    def per_block(qb, _):
        at = pl.ds(pl.multiple_of(qb * BLOCK, BLOCK), BLOCK)
        tri = lax.broadcasted_iota(jnp.int32, (BLOCK, BLOCK), 1) <= lax.broadcasted_iota(
            jnp.int32, (BLOCK, BLOCK), 0
        )
        for h in range(heads):
            query = q_ref[at, h * DH : (h + 1) * DH]
            row = h * nblk + qb
            count = counts[row]
            index = [lists[row, s] for s in range(slots)]
            parts = [jnp.where(tri, dot_t(query, block_of(k_s, qb)), NEG)]
            for base in range(0, slots, GROUP):
                block = jnp.concatenate([block_of(k_s, index[base + u]) for u in range(GROUP)], axis=0)
                scores = dot_t(query, block)
                for u in range(GROUP):
                    parts.append(
                        jnp.where(base + u < count, scores[:, u * BLOCK : (u + 1) * BLOCK], NEG)
                    )
            top = functools.reduce(jnp.maximum, parts)
            top = jnp.max(top, axis=1, keepdims=True)
            weights = jnp.exp2((parts[0] - top) * SCALE2)
            total = weights
            mixed = jnp.dot(
                weights.astype(jnp.bfloat16), block_of(v_s, qb), preferred_element_type=jnp.float32
            )
            for base in range(0, slots, GROUP):
                block = jnp.concatenate([block_of(v_s, index[base + u]) for u in range(GROUP)], axis=0)
                low = []
                for u in range(GROUP):
                    weights = jnp.exp2((parts[1 + base + u] - top) * SCALE2)
                    total = total + weights
                    low.append(weights.astype(jnp.bfloat16))
                mixed = mixed + jnp.dot(
                    jnp.concatenate(low, axis=1), block, preferred_element_type=jnp.float32
                )
            attended = mixed / jnp.sum(total, axis=1, keepdims=True)
            att[at, h * DH : (h + 1) * DH] = attended.astype(jnp.bfloat16)
        return 0

    lax.fori_loop(0, nblk, per_block, 0)
    scatter_rows(first_row, sent, dest_ref, att, out_ref)


def scatter_rows(first_row, sent, dest_ref, att, out_ref):
    shard, width = att.shape
    owners = first_row.shape[0]
    capacity = out_ref.shape[0] // owners
    batch = 16

    def per_batch(step, _):
        goal = dest_ref[...]
        place = lax.broadcasted_iota(jnp.int32, (capacity, shard), 0)
        hot = [
            jnp.where(goal - first_row[step * batch + u] == place, 1.0, 0.0).astype(jnp.bfloat16)
            for u in range(batch)
        ]
        rows = jnp.dot(jnp.concatenate(hot, axis=0), att[...], preferred_element_type=jnp.float32)
        line = lax.broadcasted_iota(jnp.int32, (capacity, width), 0)
        for u in range(batch):
            owner = step * batch + u
            kept = jnp.where(line < sent[owner], rows[u * capacity : (u + 1) * capacity], EMPTY)
            out_ref[pl.ds(pl.multiple_of(owner * capacity, capacity), capacity), :] = kept.astype(jnp.bfloat16)
        return 0

    lax.fori_loop(0, owners // batch, per_batch, 0)


def arrange_kernel(in_ref, out_ref, pick):
    shards, _, capacity, width = in_ref.shape
    slots = shards * capacity
    rows = out_ref.shape[0]
    block = in_ref[...].reshape(slots, width)

    @pl.when(pl.program_id(0) == 0)
    def _():
        used = jnp.where(block[:, :rows].astype(jnp.float32) < EMPTY / 2, 1.0, 0.0).astype(jnp.bfloat16)
        one = lax.broadcasted_iota(jnp.int32, (slots, slots), 0)
        two = lax.broadcasted_iota(jnp.int32, (slots, slots), 1)
        contract = (((0,), (0,)), ((), ()))
        before = lax.dot_general(
            used,
            jnp.where(one < two, 1.0, 0.0).astype(jnp.bfloat16),
            contract,
            preferred_element_type=jnp.float32,
        )
        here = lax.dot_general(
            used,
            jnp.where(one == two, 1.0, 0.0).astype(jnp.bfloat16),
            contract,
            preferred_element_type=jnp.float32,
        )
        line = lax.broadcasted_iota(jnp.int32, (rows, slots), 0).astype(jnp.float32)
        pick[...] = jnp.where((before == line) & (here > 0.5), 1.0, 0.0).astype(jnp.bfloat16)

    out_ref[...] = jnp.dot(pick[...], block, preferred_element_type=jnp.float32).astype(jnp.bfloat16)


def block_lists(verticals, slashes, place, nblk, nshards):
    heads = verticals.shape[0]
    query_blocks = place * nblk + jnp.arange(nblk, dtype=jnp.int32)
    vertical = jnp.broadcast_to(verticals[:, None, :], (heads, nblk, verticals.shape[1]))
    slash = query_blocks[None, :, None] - slashes[:, None, :]
    cand = jnp.concatenate([vertical, slash], axis=2)
    slots = cand.shape[2]
    order = jnp.arange(slots, dtype=jnp.int32)
    earlier = order[None, :] < order[:, None]
    repeated = jnp.any((cand[:, :, :, None] == cand[:, :, None, :]) & earlier[None, None], axis=3)
    valid = (cand >= 0) & (cand < query_blocks[None, :, None]) & jnp.logical_not(repeated)
    source = cand // nblk
    dx = (source // 2 - place // 2) % (nshards // 2)
    dz = (source - place) % 2
    piece = jnp.zeros_like(cand)
    for (ox, oz), number in PIECE.items():
        piece = jnp.where((dx == ox) & (dz == oz), number, piece)
    local = jnp.clip(piece * nblk + cand % nblk, 0, nshards * nblk - 1)
    rank = jnp.sum((valid[:, :, None, :] & earlier[None, None]).astype(jnp.int32), axis=3)
    chosen = valid[:, :, :, None] & (rank[:, :, :, None] == order)
    lists = jnp.sum(jnp.where(chosen, local[:, :, :, None], 0), axis=2)
    return lists.reshape(heads * nblk, slots), jnp.sum(valid.astype(jnp.int32), axis=2).reshape(heads * nblk)


def body(queries, keys, values, verticals, slashes, destination):
    cycle = lax.axis_size("ctx")
    groups = lax.axis_size("rows")
    place = lax.axis_index("ctx")
    group = lax.axis_index("rows")
    rows_here = queries.shape[0]
    heads = verticals.shape[0]
    nblk = rows_here // BLOCK
    devices = cycle * groups
    own_rows = rows_here // groups
    capacity = 2 * rows_here // devices
    kv_index = group * heads // (HEADS // KV_HEADS)
    core = group % 2

    own = jnp.where(
        core == 0,
        lax.dynamic_slice_in_dim(keys, kv_index * DH, DH, 1),
        lax.dynamic_slice_in_dim(values, kv_index * DH, DH, 1),
    )

    def along_x(x, step):
        return lax.ppermute(x, "ctx", [(c, (c + 2 * step) % cycle) for c in range(cycle)])

    def along_z(x):
        return lax.ppermute(x, "ctx", [(c, c ^ 1) for c in range(cycle)])

    def swap(x):
        return lax.ppermute(x, "rows", [(r, r ^ 1) for r in range(groups)])

    half = rows_here // 2
    p1 = along_x(own, 1)
    p2 = along_x(own, -1)
    p3 = along_z(own)
    p4 = along_x(p1, 1)
    p5 = along_x(p3, -1)
    p6 = along_z(p1)
    p7 = jnp.concatenate([along_x(p6[:half], 1), along_x(p5[half:], -1)], axis=0)
    mine = (p1, p2, p3, p4, p5, p6, p7)
    other = tuple(swap(x) for x in mine)

    lists, counts = block_lists(verticals, slashes, place, nblk, cycle)
    owner = destination // own_rows
    member = owner[:, None] == jnp.arange(devices, dtype=jnp.int32)[None, :]
    first_row = jnp.min(jnp.where(member, destination[:, None], ROW_CEILING), axis=0)
    sent = jnp.sum(member.astype(jnp.int32), axis=0)
    meta = jnp.stack([core, kv_index]).astype(jnp.int32)

    slots = lists.shape[1]
    outgoing = pl.pallas_call(
        functools.partial(attend_kernel, cycle, slots, heads),
        out_shape=jax.ShapeDtypeStruct((devices * capacity, heads * DH), jnp.bfloat16),
        in_specs=[SMEM] * 5 + [VMEM] * 2 + [ANY] * (2 + 2 * (cycle - 1)),
        out_specs=VMEM,
        scratch_shapes=[
            pltpu.VMEM((cycle * rows_here, DH), jnp.bfloat16),
            pltpu.VMEM((cycle * rows_here, DH), jnp.bfloat16),
            pltpu.VMEM((rows_here, heads * DH), jnp.bfloat16),
            pltpu.SemaphoreType.DMA((2 * cycle,)),
        ],
        compiler_params=pltpu.CompilerParams(vmem_limit_bytes=48 * 1024 * 1024),
        name="attend",
    )(meta, lists, counts, first_row, sent, queries, destination.reshape(1, rows_here), keys, values, *mine, *other)

    incoming = lax.all_to_all(
        outgoing.reshape(devices, capacity, heads * DH), ("ctx", "rows"), split_axis=0, concat_axis=0, tiled=True
    )
    incoming = incoming.reshape(cycle, groups, capacity, heads * DH)
    return pl.pallas_call(
        arrange_kernel,
        grid=(groups,),
        out_shape=jax.ShapeDtypeStruct((own_rows, groups * heads * DH), jnp.bfloat16),
        in_specs=[pl.BlockSpec((cycle, 1, capacity, heads * DH), lambda g: (0, g, 0, 0))],
        out_specs=pl.BlockSpec((own_rows, heads * DH), lambda g: (0, g)),
        scratch_shapes=[pltpu.VMEM((own_rows, cycle * capacity), jnp.bfloat16)],
        compiler_params=pltpu.CompilerParams(vmem_limit_bytes=32 * 1024 * 1024),
        name="arrange",
    )(incoming)


def solution(mesh):
    placed = (
        P("ctx", "rows"),
        P("ctx", None),
        P("ctx", None),
        P("rows", None),
        P("rows", None),
        P("ctx"),
    )
    return jax.shard_map(
        body, mesh=mesh, in_specs=placed, out_specs=P(("ctx", "rows"), None), check_vma=False
    )
```

```python
import functools

import jax
import jax.numpy as jnp
from jax import lax
from jax.experimental import pallas as pl
from jax.experimental.pallas import tpu as pltpu
from jax.sharding import PartitionSpec as P

HEADS = 32
KV_HEADS = 8
DH = 128
BLOCK = 128
NEG = -1e30
ROW_CEILING = 1 << 30
EMPTY = 1048576.0
SCALE2 = DH**-0.5 * 1.4426950408889634
GROUP = 4
PIECE = {
    (0, 0): (0, 0),
    (3, 0): (0, 1),
    (1, 0): (0, 2),
    (0, 1): (0, 3),
    (2, 0): (1, 0),
    (1, 1): (1, 1),
    (3, 1): (1, 2),
    (2, 1): (2, 0),
}
VISITS = 3
ANY = pl.BlockSpec(memory_space=pl.ANY)
SMEM = pl.BlockSpec(memory_space=pltpu.SMEM)
VMEM = pl.BlockSpec(memory_space=pltpu.VMEM)


def dot_t(a, b):
    return lax.dot_general(a, b, (((1,), (1,)), ((), ())), preferred_element_type=jnp.float32)


def visit_kernel(plan, meta, lists, counts, q_ref, *rest):
    first, last, pieces, halves, slots, heads, group, chains = plan
    rest = list(rest)
    take = lambda n: [rest.pop(0) for _ in range(n)]
    own = take(2) if first else []
    mine, other = take(pieces), take(pieces)
    state_in = [] if first else take(3)
    first_row, sent, dest_ref = take(3) if last else (None, None, None)
    outs = take(1) if last else take(3)
    k_s, v_s = take(2)
    att = take(1)[0] if last else None
    sem = take(1)[0]
    nblk = q_ref.shape[0] // BLOCK
    shard = q_ref.shape[0]
    size = shard // halves
    core, kv = meta[0], meta[1]
    column = pl.ds(pl.multiple_of(kv * DH, DH), DH)
    skip = len(own) // 2

    keep = []
    if first:
        for ref, to, number in ((own[0], k_s, 0), (own[1], v_s, 1)):
            copy = pltpu.make_async_copy(ref.at[:, column], to.at[pl.ds(0, shard)], sem.at[number])
            copy.start()
            keep.append(copy)
    for p in range(pieces):
        spot = pl.ds(skip * shard + p * size, size)
        number = 2 * skip + 2 * p

        @pl.when(core == 0)
        def _():
            pltpu.make_async_copy(mine[p], k_s.at[spot], sem.at[number]).start()
            pltpu.make_async_copy(other[p], v_s.at[spot], sem.at[number + 1]).start()

        @pl.when(core != 0)
        def _():
            pltpu.make_async_copy(other[p], k_s.at[spot], sem.at[number]).start()
            pltpu.make_async_copy(mine[p], v_s.at[spot], sem.at[number + 1]).start()

        keep.append(pltpu.make_async_copy(mine[p], k_s.at[spot], sem.at[number]))
        keep.append(pltpu.make_async_copy(mine[p], v_s.at[spot], sem.at[number + 1]))
    for copy in keep:
        copy.wait()

    def block_of(ref, index):
        return ref[pl.ds(pl.multiple_of(index * BLOCK, BLOCK), BLOCK), :]

    def softmax_step(state, scores, values_block):
        top, total, mixed = state
        width = scores.shape[1] // BLOCK
        parts = [scores[:, u * BLOCK : (u + 1) * BLOCK] for u in range(width)]
        peak = jnp.max(functools.reduce(jnp.maximum, parts), axis=1, keepdims=True)
        high = peak if top is None else jnp.maximum(top, peak)
        weights = [jnp.exp2((x - high) * SCALE2) for x in parts]
        low = jnp.concatenate([w.astype(jnp.bfloat16) for w in weights], axis=1)
        fresh = jnp.dot(low, values_block, preferred_element_type=jnp.float32)
        added = functools.reduce(jnp.add, weights)
        if top is None:
            return high, added, fresh
        factor = jnp.exp2((top - high) * SCALE2)
        return high, total * factor + added, mixed * factor + fresh

    def per_step(step, _):
        pairs = [(step * chains + b, h) for b in range(chains) for h in range(heads)]
        blocks = [pl.ds(pl.multiple_of(qb * BLOCK, BLOCK), BLOCK) for qb, _ in pairs]
        lanes = [slice(h * DH, (h + 1) * DH) for _, h in pairs]
        rows = [h * nblk + qb for qb, h in pairs]
        queries = [q_ref[at, lane] for at, lane in zip(blocks, lanes)]
        state = []
        for i, (qb, h) in enumerate(pairs):
            if first:
                tri = lax.broadcasted_iota(jnp.int32, (BLOCK, BLOCK), 1) <= lax.broadcasted_iota(
                    jnp.int32, (BLOCK, BLOCK), 0
                )
                scores = jnp.where(tri, dot_t(queries[i], block_of(k_s, qb)), NEG)
                state.append(softmax_step((None, None, None), scores, block_of(v_s, qb)))
            else:
                state.append(
                    (
                        state_in[0][blocks[i], lanes[i]][:, :1],
                        state_in[1][blocks[i], lanes[i]],
                        state_in[2][blocks[i], lanes[i]],
                    )
                )
        number = [counts[row] for row in rows]
        most = functools.reduce(jnp.maximum, number)

        def per_group(j, state):
            fresh = []
            for i in range(len(pairs)):
                index = [lists[rows[i], j * group + u] for u in range(group)]
                keys_block = jnp.concatenate([block_of(k_s, x) for x in index], axis=0)
                scores = dot_t(queries[i], keys_block)
                scores = jnp.concatenate(
                    [
                        jnp.where(j * group + u < number[i], scores[:, u * BLOCK : (u + 1) * BLOCK], NEG)
                        for u in range(group)
                    ],
                    axis=1,
                )
                values_block = jnp.concatenate([block_of(v_s, x) for x in index], axis=0)
                fresh.append(softmax_step(state[i], scores, values_block))
            return tuple(fresh)

        state = lax.fori_loop(0, (most + group - 1) // group, per_group, tuple(state))
        for i in range(len(pairs)):
            top, total, mixed = state[i]
            if last:
                attended = mixed / jnp.sum(total, axis=1, keepdims=True)
                att[blocks[i], lanes[i]] = attended.astype(jnp.bfloat16)
            else:
                outs[0][blocks[i], lanes[i]] = jnp.broadcast_to(top, (BLOCK, DH))
                outs[1][blocks[i], lanes[i]] = total
                outs[2][blocks[i], lanes[i]] = mixed
        return 0

    lax.fori_loop(0, nblk // chains, per_step, 0)
    if last:
        scatter_rows(first_row, sent, dest_ref, att, outs[0])


def visit(first, last, group, chains, meta, lists, counts, queries, own, mine, other, state, final):
    shard, width = queries.shape
    heads = width // DH
    pieces = len(mine)
    halves = shard // mine[0].shape[0]
    slots = lists.shape[1]
    held = (len(own) // 2) * shard + sum(x.shape[0] for x in mine)
    plan = (first, last, pieces, halves, slots, heads, group, chains)
    if last:
        out_shape = jax.ShapeDtypeStruct((final[3], width), jnp.bfloat16)
        out_specs = VMEM
    else:
        out_shape = [jax.ShapeDtypeStruct((shard, width), jnp.float32)] * 3
        out_specs = [VMEM] * 3
    scratch = [pltpu.VMEM((held, DH), jnp.bfloat16)] * 2
    if last:
        scratch.append(pltpu.VMEM((shard, width), jnp.bfloat16))
    scratch.append(pltpu.SemaphoreType.DMA((len(own) + 2 * pieces,)))
    return pl.pallas_call(
        functools.partial(visit_kernel, plan),
        out_shape=out_shape,
        in_specs=[SMEM] * 3
        + [VMEM]
        + [ANY] * (len(own) + 2 * pieces)
        + [VMEM] * len(state)
        + ([SMEM, SMEM, VMEM] if last else []),
        out_specs=out_specs,
        scratch_shapes=scratch,
        compiler_params=pltpu.CompilerParams(vmem_limit_bytes=40 * 1024 * 1024),
        cost_estimate=pl.CostEstimate(
            flops=held * width * 16 * DH, bytes_accessed=16 * 1024 * 1024, transcendentals=held * 4096
        ),
        name="visit_last" if last else "visit_first" if first else "visit_next",
    )(meta, lists, counts, queries, *own, *mine, *other, *state, *(final[:3] if last else ()))


def scatter_rows(first_row, sent, dest_ref, att, out_ref):
    shard, width = att.shape
    owners = first_row.shape[0]
    capacity = out_ref.shape[0] // owners
    batch = 16

    def per_batch(step, _):
        goal = dest_ref[...]
        place = lax.broadcasted_iota(jnp.int32, (capacity, shard), 0)
        hot = [
            jnp.where(goal - first_row[step * batch + u] == place, 1.0, 0.0).astype(jnp.bfloat16)
            for u in range(batch)
        ]
        rows = jnp.dot(jnp.concatenate(hot, axis=0), att[...], preferred_element_type=jnp.float32)
        line = lax.broadcasted_iota(jnp.int32, (capacity, width), 0)
        for u in range(batch):
            owner = step * batch + u
            kept = jnp.where(line < sent[owner], rows[u * capacity : (u + 1) * capacity], EMPTY)
            out_ref[pl.ds(pl.multiple_of(owner * capacity, capacity), capacity), :] = kept.astype(jnp.bfloat16)
        return 0

    lax.fori_loop(0, owners // batch, per_batch, 0)


def arrange_kernel(in_ref, out_ref, pick):
    shards, _, capacity, width = in_ref.shape
    slots = shards * capacity
    rows = out_ref.shape[0]
    block = in_ref[...].reshape(slots, width)

    @pl.when(pl.program_id(0) == 0)
    def _():
        used = jnp.where(block[:, :rows].astype(jnp.float32) < EMPTY / 2, 1.0, 0.0).astype(jnp.bfloat16)
        one = lax.broadcasted_iota(jnp.int32, (slots, slots), 0)
        two = lax.broadcasted_iota(jnp.int32, (slots, slots), 1)
        contract = (((0,), (0,)), ((), ()))
        before = lax.dot_general(
            used,
            jnp.where(one < two, 1.0, 0.0).astype(jnp.bfloat16),
            contract,
            preferred_element_type=jnp.float32,
        )
        here = lax.dot_general(
            used,
            jnp.where(one == two, 1.0, 0.0).astype(jnp.bfloat16),
            contract,
            preferred_element_type=jnp.float32,
        )
        line = lax.broadcasted_iota(jnp.int32, (rows, slots), 0).astype(jnp.float32)
        pick[...] = jnp.where((before == line) & (here > 0.5), 1.0, 0.0).astype(jnp.bfloat16)

    out_ref[...] = jnp.dot(pick[...], block, preferred_element_type=jnp.float32).astype(jnp.bfloat16)


def block_lists(verticals, slashes, place, nblk, nshards):
    heads = verticals.shape[0]
    query_blocks = place * nblk + jnp.arange(nblk, dtype=jnp.int32)
    vertical = jnp.broadcast_to(verticals[:, None, :], (heads, nblk, verticals.shape[1]))
    slash = query_blocks[None, :, None] - slashes[:, None, :]
    cand = jnp.concatenate([vertical, slash], axis=2)
    slots = cand.shape[2]
    order = jnp.arange(slots, dtype=jnp.int32)
    earlier = order[None, :] < order[:, None]
    repeated = jnp.any((cand[:, :, :, None] == cand[:, :, None, :]) & earlier[None, None], axis=3)
    valid = (cand >= 0) & (cand < query_blocks[None, :, None]) & jnp.logical_not(repeated)
    source = cand // nblk
    dx = (source // 2 - place // 2) % (nshards // 2)
    dz = (source - place) % 2
    piece = jnp.zeros_like(cand)
    when = jnp.zeros_like(cand)
    for (ox, oz), (number, position) in PIECE.items():
        here = (dx == ox) & (dz == oz)
        piece = jnp.where(here, position, piece)
        when = jnp.where(here, number, when)
    local = piece * nblk + cand % nblk
    valid = valid[None] & (when[None] == jnp.arange(VISITS, dtype=jnp.int32)[:, None, None, None])
    rank = jnp.sum((valid[:, :, :, None, :] & earlier).astype(jnp.int32), axis=4)
    chosen = valid[:, :, :, :, None] & (rank[:, :, :, :, None] == order)
    lists = jnp.sum(jnp.where(chosen, local[None, :, :, :, None], 0), axis=3)
    lists = lists.reshape(VISITS, heads * nblk, slots)
    counts = jnp.sum(valid.astype(jnp.int32), axis=3).reshape(VISITS, heads * nblk)
    return lists, counts


def body(queries, keys, values, verticals, slashes, destination):
    cycle = lax.axis_size("ctx")
    groups = lax.axis_size("rows")
    place = lax.axis_index("ctx")
    group = lax.axis_index("rows")
    rows_here = queries.shape[0]
    heads = verticals.shape[0]
    nblk = rows_here // BLOCK
    devices = cycle * groups
    own_rows = rows_here // groups
    capacity = 2 * rows_here // devices
    kv_index = group * heads // (HEADS // KV_HEADS)
    core = group % 2

    own = jnp.where(
        core == 0,
        lax.dynamic_slice_in_dim(keys, kv_index * DH, DH, 1),
        lax.dynamic_slice_in_dim(values, kv_index * DH, DH, 1),
    )

    def along_x(x, step):
        return lax.ppermute(x, "ctx", [(c, (c + 2 * step) % cycle) for c in range(cycle)])

    def along_z(x):
        return lax.ppermute(x, "ctx", [(c, c ^ 1) for c in range(cycle)])

    def swap(x):
        return lax.ppermute(x, "rows", [(r, r ^ 1) for r in range(groups)])

    half = rows_here // 2
    p1 = along_x(own, 1)
    p2 = along_x(own, -1)
    p3 = along_z(own)
    p4 = along_x(p1, 1)
    p5 = along_x(p3, -1)
    p6 = along_z(p1)
    p7 = along_x(p6[:half], 1)
    p8 = along_x(p5[half:], -1)

    lists, counts = block_lists(verticals, slashes, place, nblk, cycle)
    owner = destination // own_rows
    member = owner[:, None] == jnp.arange(devices, dtype=jnp.int32)[None, :]
    first_row = jnp.min(jnp.where(member, destination[:, None], ROW_CEILING), axis=0)
    sent = jnp.sum(member.astype(jnp.int32), axis=0)
    meta = jnp.stack([core, kv_index]).astype(jnp.int32)

    state = visit(
        True, False, 4, 1, meta, lists[0], counts[0], queries, (keys, values),
        (p1, p2, p3), (swap(p1), swap(p2), swap(p3)), (), (),
    )
    state = visit(
        False, False, 4, 1, meta, lists[1], counts[1], queries, (),
        (p4, p5, p6), (swap(p4), swap(p5), swap(p6)), state, (),
    )
    final = (first_row, sent, destination.reshape(1, rows_here), devices * capacity)
    outgoing = visit(
        False, True, 2, 1, meta, lists[2], counts[2], queries, (), (p7, p8), (swap(p7), swap(p8)), state, final
    )

    incoming = lax.all_to_all(
        outgoing.reshape(devices, capacity, heads * DH), ("ctx", "rows"), split_axis=0, concat_axis=0, tiled=True
    )
    incoming = incoming.reshape(cycle, groups, capacity, heads * DH)
    return pl.pallas_call(
        arrange_kernel,
        grid=(groups,),
        out_shape=jax.ShapeDtypeStruct((own_rows, groups * heads * DH), jnp.bfloat16),
        in_specs=[pl.BlockSpec((cycle, 1, capacity, heads * DH), lambda g: (0, g, 0, 0))],
        out_specs=pl.BlockSpec((own_rows, heads * DH), lambda g: (0, g)),
        scratch_shapes=[pltpu.VMEM((own_rows, cycle * capacity), jnp.bfloat16)],
        compiler_params=pltpu.CompilerParams(vmem_limit_bytes=32 * 1024 * 1024),
        name="arrange",
    )(incoming)


def solution(mesh):
    placed = (
        P("ctx", "rows"),
        P("ctx", None),
        P("ctx", None),
        P("rows", None),
        P("rows", None),
        P("ctx"),
    )
    return jax.shard_map(
        body, mesh=mesh, in_specs=placed, out_specs=P(("ctx", "rows"), None), check_vma=False
    )
```

```python
import functools

import jax
import jax.numpy as jnp
from jax import lax
from jax.experimental import pallas as pl
from jax.experimental.pallas import tpu as pltpu
from jax.sharding import PartitionSpec as P

HEADS = 32
KV_HEADS = 8
DH = 128
BLOCK = 128
NEG = -1e30
ROW_CEILING = 1 << 30
EMPTY = 1048576.0
SCALE2 = DH**-0.5 * 1.4426950408889634
GROUP = 4
SLOT = 32
PIECE = {(0, 0): 0, (3, 0): 1, (1, 0): 2, (0, 1): 3, (2, 0): 4, (1, 1): 5, (3, 1): 6, (2, 1): 7}
ANY = pl.BlockSpec(memory_space=pl.ANY)
SMEM = pl.BlockSpec(memory_space=pltpu.SMEM)
VMEM = pl.BlockSpec(memory_space=pltpu.VMEM)


def dot_t(a, b):
    return lax.dot_general(a, b, (((1,), (1,)), ((), ())), preferred_element_type=jnp.float32)


def attend_kernel(sizes, slots, heads, meta, lists, counts, first_row, sent, q_ref, dest_ref, keys, values, *rest):
    pieces = len(sizes)
    mine, other = rest[:pieces], rest[pieces : 2 * pieces]
    out_ref, k_s, v_s, att, sem = rest[2 * pieces :]
    shard = q_ref.shape[0]
    nblk = shard // BLOCK
    core, kv = meta[0], meta[1]
    column = pl.ds(pl.multiple_of(kv * DH, DH), DH)
    copies = []
    for ref, to in ((keys, k_s), (values, v_s)):
        copy = pltpu.make_async_copy(ref.at[:, column], to.at[pl.ds(0, shard)], sem.at[len(copies)])
        copy.start()
        copies.append(copy)
    begin = shard
    for p in range(pieces):
        spot = pl.ds(begin, sizes[p])
        begin += sizes[p]
        number = len(copies)

        @pl.when(core == 0)
        def _():
            pltpu.make_async_copy(mine[p], k_s.at[spot], sem.at[number]).start()
            pltpu.make_async_copy(other[p], v_s.at[spot], sem.at[number + 1]).start()

        @pl.when(core != 0)
        def _():
            pltpu.make_async_copy(other[p], k_s.at[spot], sem.at[number]).start()
            pltpu.make_async_copy(mine[p], v_s.at[spot], sem.at[number + 1]).start()

        copies.append(pltpu.make_async_copy(mine[p], k_s.at[spot], sem.at[number]))
        copies.append(pltpu.make_async_copy(mine[p], v_s.at[spot], sem.at[number + 1]))
    for copy in copies:
        copy.wait()

    def block_of(ref, index):
        return ref[pl.ds(pl.multiple_of(index * BLOCK, BLOCK), BLOCK), :]

    def per_block(qb, _):
        at = pl.ds(pl.multiple_of(qb * BLOCK, BLOCK), BLOCK)
        tri = lax.broadcasted_iota(jnp.int32, (BLOCK, BLOCK), 1) <= lax.broadcasted_iota(
            jnp.int32, (BLOCK, BLOCK), 0
        )
        for h in range(heads):
            query = q_ref[at, h * DH : (h + 1) * DH]
            row = h * nblk + qb
            count = counts[row]
            index = [lists[row, s] for s in range(slots)]
            parts = [jnp.where(tri, dot_t(query, block_of(k_s, qb)), NEG)]
            for base in range(0, slots, GROUP):
                block = jnp.concatenate([block_of(k_s, index[base + u]) for u in range(GROUP)], axis=0)
                scores = dot_t(query, block)
                for u in range(GROUP):
                    parts.append(
                        jnp.where(base + u < count, scores[:, u * BLOCK : (u + 1) * BLOCK], NEG)
                    )
            top = functools.reduce(jnp.maximum, parts)
            top = jnp.max(top, axis=1, keepdims=True)
            weights = jnp.exp2((parts[0] - top) * SCALE2)
            total = weights
            mixed = jnp.dot(
                weights.astype(jnp.bfloat16), block_of(v_s, qb), preferred_element_type=jnp.float32
            )
            for base in range(0, slots, GROUP):
                block = jnp.concatenate([block_of(v_s, index[base + u]) for u in range(GROUP)], axis=0)
                low = []
                for u in range(GROUP):
                    weights = jnp.exp2((parts[1 + base + u] - top) * SCALE2)
                    total = total + weights
                    low.append(weights.astype(jnp.bfloat16))
                mixed = mixed + jnp.dot(
                    jnp.concatenate(low, axis=1), block, preferred_element_type=jnp.float32
                )
            attended = mixed / jnp.sum(total, axis=1, keepdims=True)
            att[at, h * DH : (h + 1) * DH] = attended.astype(jnp.bfloat16)
        return 0

    lax.fori_loop(0, nblk, per_block, 0)
    scatter_rows(first_row, sent, dest_ref, att, out_ref)


def scatter_rows(first_row, sent, dest_ref, att, out_ref):
    shard, width = att.shape
    owners = first_row.shape[0]
    capacity = out_ref.shape[0] // owners
    batch = 16

    def per_batch(step, _):
        goal = dest_ref[...]
        place = lax.broadcasted_iota(jnp.int32, (capacity, shard), 0)
        hot = [
            jnp.where(goal - first_row[step * batch + u] == place, 1.0, 0.0).astype(jnp.bfloat16)
            for u in range(batch)
        ]
        rows = jnp.dot(jnp.concatenate(hot, axis=0), att[...], preferred_element_type=jnp.float32)
        line = lax.broadcasted_iota(jnp.int32, (capacity, width), 0)
        for u in range(batch):
            owner = step * batch + u
            kept = jnp.where(line < sent[owner], rows[u * capacity : (u + 1) * capacity], EMPTY)
            out_ref[pl.ds(pl.multiple_of(owner * capacity, capacity), capacity), :] = kept.astype(jnp.bfloat16)
        return 0

    lax.fori_loop(0, owners // batch, per_batch, 0)


def arrange_kernel(in_ref, out_ref):
    shards, groups, capacity, width = in_ref.shape
    slots = shards * capacity
    rows = out_ref.shape[0]
    block = in_ref[:, 0].reshape(slots, width)
    used = jnp.where(block[:, :rows].astype(jnp.float32) < EMPTY / 2, 1.0, 0.0).astype(jnp.bfloat16)
    one = lax.broadcasted_iota(jnp.int32, (slots, slots), 0)
    two = lax.broadcasted_iota(jnp.int32, (slots, slots), 1)
    contract = (((0,), (0,)), ((), ()))
    before = lax.dot_general(
        used, jnp.where(one < two, 1.0, 0.0).astype(jnp.bfloat16), contract, preferred_element_type=jnp.float32
    )
    here = lax.dot_general(
        used, jnp.where(one == two, 1.0, 0.0).astype(jnp.bfloat16), contract, preferred_element_type=jnp.float32
    )
    line = lax.broadcasted_iota(jnp.int32, (rows, slots), 0).astype(jnp.float32)
    pick = jnp.where((before == line) & (here > 0.5), 1.0, 0.0).astype(jnp.bfloat16)
    for g in range(groups):
        block = in_ref[:, g].reshape(slots, width)
        out_ref[:, g * width : (g + 1) * width] = jnp.dot(pick, block, preferred_element_type=jnp.float32).astype(
            jnp.bfloat16
        )


def block_lists(verticals, slashes, place, nblk, nshards):
    heads = verticals.shape[0]
    query_blocks = place * nblk + jnp.arange(nblk, dtype=jnp.int32)
    vertical = jnp.broadcast_to(verticals[:, None, :], (heads, nblk, verticals.shape[1]))
    slash = query_blocks[None, :, None] - slashes[:, None, :]
    cand = jnp.concatenate([vertical, slash], axis=2)
    slots = cand.shape[2]
    order = jnp.arange(slots, dtype=jnp.int32)
    earlier = order[None, :] < order[:, None]
    repeated = jnp.any((cand[:, :, :, None] == cand[:, :, None, :]) & earlier[None, None], axis=3)
    valid = (cand >= 0) & (cand < query_blocks[None, :, None]) & jnp.logical_not(repeated)
    source = cand // nblk
    dx = (source // 2 - place // 2) % (nshards // 2)
    dz = (source - place) % 2
    piece = jnp.zeros_like(cand)
    for (ox, oz), number in PIECE.items():
        piece = jnp.where((dx == ox) & (dz == oz), number, piece)
    local = jnp.clip(piece * nblk + cand % nblk, 0, nshards * nblk - 1)
    rank = jnp.sum((valid[:, :, None, :] & earlier[None, None]).astype(jnp.int32), axis=3)
    chosen = valid[:, :, :, None] & (rank[:, :, :, None] == order)
    lists = jnp.sum(jnp.where(chosen, local[:, :, :, None], 0), axis=2)
    return lists.reshape(heads * nblk, slots), jnp.sum(valid.astype(jnp.int32), axis=2).reshape(heads * nblk)


def body(queries, keys, values, verticals, slashes, destination):
    cycle = lax.axis_size("ctx")
    groups = lax.axis_size("rows")
    place = lax.axis_index("ctx")
    group = lax.axis_index("rows")
    rows_here = queries.shape[0]
    heads = verticals.shape[0]
    nblk = rows_here // BLOCK
    devices = cycle * groups
    own_rows = rows_here // groups
    capacity = SLOT
    kv_index = group * heads // (HEADS // KV_HEADS)
    core = group % 2

    own = jnp.where(
        core == 0,
        lax.dynamic_slice_in_dim(keys, kv_index * DH, DH, 1),
        lax.dynamic_slice_in_dim(values, kv_index * DH, DH, 1),
    )

    def along_x(x, step):
        return lax.ppermute(x, "ctx", [(c, (c + 2 * step) % cycle) for c in range(cycle)])

    def along_z(x):
        return lax.ppermute(x, "ctx", [(c, c ^ 1) for c in range(cycle)])

    def swap(x):
        return lax.ppermute(x, "rows", [(r, r ^ 1) for r in range(groups)])

    half = rows_here // 2
    p1 = along_x(own, 1)
    p2 = along_x(own, -1)
    p3 = along_z(own)
    p4 = along_x(p1, 1)
    p5 = along_x(p3, -1)
    p6 = along_z(p1)
    p1, p2, p3, p4, p5, p6 = lax.optimization_barrier((p1, p2, p3, p4, p5, p6))
    p7 = along_x(p6[:half], 1)
    p8 = along_x(p5[half:], -1)
    mine = (p1, p2, p3, p4, p5, p6, p7, p8)
    other = tuple(swap(x) for x in mine)

    lists, counts = block_lists(verticals, slashes, place, nblk, cycle)
    owner = destination // own_rows
    member = owner[:, None] == jnp.arange(devices, dtype=jnp.int32)[None, :]
    first_row = jnp.min(jnp.where(member, destination[:, None], ROW_CEILING), axis=0)
    sent = jnp.sum(member.astype(jnp.int32), axis=0)
    meta = jnp.stack([core, kv_index]).astype(jnp.int32)

    slots = lists.shape[1]
    outgoing = pl.pallas_call(
        functools.partial(attend_kernel, [x.shape[0] for x in mine], slots, heads),
        out_shape=jax.ShapeDtypeStruct((devices * capacity, heads * DH), jnp.bfloat16),
        in_specs=[SMEM] * 5 + [VMEM] * 2 + [ANY] * (2 + 2 * len(mine)),
        out_specs=VMEM,
        scratch_shapes=[
            pltpu.VMEM((cycle * rows_here, DH), jnp.bfloat16),
            pltpu.VMEM((cycle * rows_here, DH), jnp.bfloat16),
            pltpu.VMEM((rows_here, heads * DH), jnp.bfloat16),
            pltpu.SemaphoreType.DMA((2 + 2 * len(mine),)),
        ],
        compiler_params=pltpu.CompilerParams(vmem_limit_bytes=60 * 1024 * 1024),
        name="attend",
    )(meta, lists, counts, first_row, sent, queries, destination.reshape(1, rows_here), keys, values, *mine, *other)

    incoming = lax.all_to_all(
        outgoing.reshape(devices, capacity, heads * DH), ("ctx", "rows"), split_axis=0, concat_axis=0, tiled=True
    )
    incoming = incoming.reshape(cycle, groups, capacity, heads * DH)
    return pl.pallas_call(
        arrange_kernel,
        out_shape=jax.ShapeDtypeStruct((own_rows, groups * heads * DH), jnp.bfloat16),
        in_specs=[VMEM],
        out_specs=VMEM,
        compiler_params=pltpu.CompilerParams(vmem_limit_bytes=60 * 1024 * 1024),
        name="arrange",
    )(incoming)


def solution(mesh):
    placed = (
        P("ctx", "rows"),
        P("ctx", None),
        P("ctx", None),
        P("rows", None),
        P("rows", None),
        P("ctx"),
    )
    return jax.shard_map(
        body, mesh=mesh, in_specs=placed, out_specs=P(("ctx", "rows"), None), check_vma=False
    )
```

```python
import functools

import jax
import jax.numpy as jnp
from jax import lax
from jax.experimental import pallas as pl
from jax.experimental.pallas import tpu as pltpu
from jax.sharding import PartitionSpec as P

HEADS = 32
KV_HEADS = 8
DH = 128
BLOCK = 128
NEG = -1e30
ROW_CEILING = 1 << 30
EMPTY = 1048576.0
SCALE2 = DH**-0.5 * 1.4426950408889634
GROUP = 4
SLOT = 32
PIECE = {(0, 0): 0, (3, 0): 1, (1, 0): 2, (0, 1): 3, (2, 0): 4, (1, 1): 5, (3, 1): 6, (2, 1): 7}
ANY = pl.BlockSpec(memory_space=pl.ANY)
SMEM = pl.BlockSpec(memory_space=pltpu.SMEM)
VMEM = pl.BlockSpec(memory_space=pltpu.VMEM)


def dot_t(a, b):
    return lax.dot_general(a, b, (((1,), (1,)), ((), ())), preferred_element_type=jnp.float32)


def attend_kernel(sizes, slots, heads, meta, lists, counts, first_row, sent, q_ref, dest_ref, keys, values, *rest):
    pieces = len(sizes)
    mine, other = rest[:pieces], rest[pieces : 2 * pieces]
    out_ref, k_s, v_s, att, sem = rest[2 * pieces :]
    shard = q_ref.shape[0]
    nblk = shard // BLOCK
    core, kv = meta[0], meta[1]
    column = pl.ds(pl.multiple_of(kv * DH, DH), DH)
    copies = []
    for ref, to in ((keys, k_s), (values, v_s)):
        copy = pltpu.make_async_copy(ref.at[:, column], to.at[pl.ds(0, shard)], sem.at[len(copies)])
        copy.start()
        copies.append(copy)
    begin = shard
    for p in range(pieces):
        spot = pl.ds(begin, sizes[p])
        begin += sizes[p]
        number = len(copies)

        @pl.when(core == 0)
        def _():
            pltpu.make_async_copy(mine[p], k_s.at[spot], sem.at[number]).start()
            pltpu.make_async_copy(other[p], v_s.at[spot], sem.at[number + 1]).start()

        @pl.when(core != 0)
        def _():
            pltpu.make_async_copy(other[p], k_s.at[spot], sem.at[number]).start()
            pltpu.make_async_copy(mine[p], v_s.at[spot], sem.at[number + 1]).start()

        copies.append(pltpu.make_async_copy(mine[p], k_s.at[spot], sem.at[number]))
        copies.append(pltpu.make_async_copy(mine[p], v_s.at[spot], sem.at[number + 1]))
    for copy in copies:
        copy.wait()

    def block_of(ref, index):
        return ref[pl.ds(pl.multiple_of(index * BLOCK, BLOCK), BLOCK), :]

    def per_block(qb, _):
        at = pl.ds(pl.multiple_of(qb * BLOCK, BLOCK), BLOCK)
        tri = lax.broadcasted_iota(jnp.int32, (BLOCK, BLOCK), 1) <= lax.broadcasted_iota(
            jnp.int32, (BLOCK, BLOCK), 0
        )
        for h in range(heads):
            query = q_ref[at, h * DH : (h + 1) * DH]
            row = h * nblk + qb
            count = counts[row]
            index = [lists[row, s] for s in range(slots)]
            parts = [jnp.where(tri, dot_t(query, block_of(k_s, qb)), NEG)]
            for base in range(0, slots, GROUP):
                block = jnp.concatenate([block_of(k_s, index[base + u]) for u in range(GROUP)], axis=0)
                scores = dot_t(query, block)
                for u in range(GROUP):
                    parts.append(
                        jnp.where(base + u < count, scores[:, u * BLOCK : (u + 1) * BLOCK], NEG)
                    )
            top = functools.reduce(jnp.maximum, parts)
            top = jnp.max(top, axis=1, keepdims=True)
            weights = jnp.exp2((parts[0] - top) * SCALE2)
            total = weights
            mixed = jnp.dot(
                weights.astype(jnp.bfloat16), block_of(v_s, qb), preferred_element_type=jnp.float32
            )
            for base in range(0, slots, GROUP):
                block = jnp.concatenate([block_of(v_s, index[base + u]) for u in range(GROUP)], axis=0)
                low = []
                for u in range(GROUP):
                    weights = jnp.exp2((parts[1 + base + u] - top) * SCALE2)
                    total = total + weights
                    low.append(weights.astype(jnp.bfloat16))
                mixed = mixed + jnp.dot(
                    jnp.concatenate(low, axis=1), block, preferred_element_type=jnp.float32
                )
            attended = mixed / jnp.sum(total, axis=1, keepdims=True)
            att[at, h * DH : (h + 1) * DH] = attended.astype(jnp.bfloat16)
        return 0

    lax.fori_loop(0, nblk, per_block, 0)
    scatter_rows(first_row, sent, dest_ref, att, out_ref)


def scatter_rows(first_row, sent, dest_ref, att, out_ref):
    shard, width = att.shape
    owners = first_row.shape[0]
    capacity = out_ref.shape[0] // owners
    batch = 16

    def per_batch(step, _):
        goal = dest_ref[...]
        place = lax.broadcasted_iota(jnp.int32, (capacity, shard), 0)
        hot = [
            jnp.where(goal - first_row[step * batch + u] == place, 1.0, 0.0).astype(jnp.bfloat16)
            for u in range(batch)
        ]
        rows = jnp.dot(jnp.concatenate(hot, axis=0), att[...], preferred_element_type=jnp.float32)
        line = lax.broadcasted_iota(jnp.int32, (capacity, width), 0)
        for u in range(batch):
            owner = step * batch + u
            kept = jnp.where(line < sent[owner], rows[u * capacity : (u + 1) * capacity], EMPTY)
            out_ref[pl.ds(pl.multiple_of(owner * capacity, capacity), capacity), :] = kept.astype(jnp.bfloat16)
        return 0

    lax.fori_loop(0, owners // batch, per_batch, 0)


def arrange_kernel(in_ref, out_ref):
    shards, groups, capacity, width = in_ref.shape
    slots = shards * capacity
    rows = out_ref.shape[0]
    block = in_ref[:, 0].reshape(slots, width)
    used = jnp.where(block[:, :rows].astype(jnp.float32) < EMPTY / 2, 1.0, 0.0).astype(jnp.bfloat16)
    one = lax.broadcasted_iota(jnp.int32, (slots, slots), 0)
    two = lax.broadcasted_iota(jnp.int32, (slots, slots), 1)
    contract = (((0,), (0,)), ((), ()))
    before = lax.dot_general(
        used, jnp.where(one < two, 1.0, 0.0).astype(jnp.bfloat16), contract, preferred_element_type=jnp.float32
    )
    here = lax.dot_general(
        used, jnp.where(one == two, 1.0, 0.0).astype(jnp.bfloat16), contract, preferred_element_type=jnp.float32
    )
    line = lax.broadcasted_iota(jnp.int32, (rows, slots), 0).astype(jnp.float32)
    pick = jnp.where((before == line) & (here > 0.5), 1.0, 0.0).astype(jnp.bfloat16)
    for g in range(groups):
        block = in_ref[:, g].reshape(slots, width)
        out_ref[:, g * width : (g + 1) * width] = jnp.dot(pick, block, preferred_element_type=jnp.float32).astype(
            jnp.bfloat16
        )


def block_lists(verticals, slashes, place, nblk, nshards):
    heads = verticals.shape[0]
    query_blocks = place * nblk + jnp.arange(nblk, dtype=jnp.int32)
    vertical = jnp.broadcast_to(verticals[:, None, :], (heads, nblk, verticals.shape[1]))
    slash = query_blocks[None, :, None] - slashes[:, None, :]
    cand = jnp.concatenate([vertical, slash], axis=2)
    slots = cand.shape[2]
    order = jnp.arange(slots, dtype=jnp.int32)
    earlier = order[None, :] < order[:, None]
    repeated = jnp.any((cand[:, :, :, None] == cand[:, :, None, :]) & earlier[None, None], axis=3)
    valid = (cand >= 0) & (cand < query_blocks[None, :, None]) & jnp.logical_not(repeated)
    source = cand // nblk
    dx = (source // 2 - place // 2) % (nshards // 2)
    dz = (source - place) % 2
    piece = jnp.zeros_like(cand)
    for (ox, oz), number in PIECE.items():
        piece = jnp.where((dx == ox) & (dz == oz), number, piece)
    local = jnp.clip(piece * nblk + cand % nblk, 0, nshards * nblk - 1)
    rank = jnp.sum((valid[:, :, None, :] & earlier[None, None]).astype(jnp.int32), axis=3)
    chosen = valid[:, :, :, None] & (rank[:, :, :, None] == order)
    lists = jnp.sum(jnp.where(chosen, local[:, :, :, None], 0), axis=2)
    return lists.reshape(heads * nblk, slots), jnp.sum(valid.astype(jnp.int32), axis=2).reshape(heads * nblk)


def body(queries, keys, values, verticals, slashes, destination):
    cycle = lax.axis_size("ctx")
    groups = lax.axis_size("rows")
    place = lax.axis_index("ctx")
    group = lax.axis_index("rows")
    rows_here = queries.shape[0]
    heads = verticals.shape[0]
    nblk = rows_here // BLOCK
    devices = cycle * groups
    own_rows = rows_here // groups
    capacity = SLOT
    kv_index = group * heads // (HEADS // KV_HEADS)
    core = group % 2

    own = jnp.where(
        core == 0,
        lax.dynamic_slice_in_dim(keys, kv_index * DH, DH, 1),
        lax.dynamic_slice_in_dim(values, kv_index * DH, DH, 1),
    )

    def along_x(x, step):
        return lax.ppermute(x, "ctx", [(c, (c + 2 * step) % cycle) for c in range(cycle)])

    def along_z(x):
        return lax.ppermute(x, "ctx", [(c, c ^ 1) for c in range(cycle)])

    def swap(x):
        return lax.ppermute(x, "rows", [(r, r ^ 1) for r in range(groups)])

    half = rows_here // 2
    p1 = along_x(own, 1)
    p2 = along_x(own, -1)
    p3 = along_z(own)

    lists, counts = block_lists(verticals, slashes, place, nblk, cycle)
    owner = destination // own_rows
    member = owner[:, None] == jnp.arange(devices, dtype=jnp.int32)[None, :]
    first_row = jnp.min(jnp.where(member, destination[:, None], ROW_CEILING), axis=0)
    sent = jnp.sum(member.astype(jnp.int32), axis=0)
    meta = jnp.stack([core, kv_index]).astype(jnp.int32)
    small = (meta, lists, counts, first_row, sent)
    p1, p3, small = lax.optimization_barrier((p1, p3, small))

    p4 = along_x(p1, 1)
    p5 = along_x(p3, -1)
    p6 = along_z(p1)
    mine = [jnp.concatenate([p1, p2, p3], axis=0)]
    other = [swap(mine[0])]
    p7 = along_x(p6[:half], 1)
    p8 = along_x(p5[half:], -1)
    mine += [jnp.concatenate([p4, p5, p6], axis=0), p7, p8]
    other += [swap(x) for x in mine[1:]]

    slots = lists.shape[1]
    outgoing = pl.pallas_call(
        functools.partial(attend_kernel, [x.shape[0] for x in mine], slots, heads),
        out_shape=jax.ShapeDtypeStruct((devices * capacity, heads * DH), jnp.bfloat16),
        in_specs=[SMEM] * 5 + [VMEM] * 2 + [ANY] * (2 + 2 * len(mine)),
        out_specs=VMEM,
        scratch_shapes=[
            pltpu.VMEM((cycle * rows_here, DH), jnp.bfloat16),
            pltpu.VMEM((cycle * rows_here, DH), jnp.bfloat16),
            pltpu.VMEM((rows_here, heads * DH), jnp.bfloat16),
            pltpu.SemaphoreType.DMA((2 + 2 * len(mine),)),
        ],
        compiler_params=pltpu.CompilerParams(vmem_limit_bytes=60 * 1024 * 1024),
        name="attend",
    )(*small, queries, destination.reshape(1, rows_here), keys, values, *mine, *other)

    incoming = lax.all_to_all(
        outgoing.reshape(devices, capacity, heads * DH), ("ctx", "rows"), split_axis=0, concat_axis=0, tiled=True
    )
    incoming = incoming.reshape(cycle, groups, capacity, heads * DH)
    return pl.pallas_call(
        arrange_kernel,
        out_shape=jax.ShapeDtypeStruct((own_rows, groups * heads * DH), jnp.bfloat16),
        in_specs=[VMEM],
        out_specs=VMEM,
        compiler_params=pltpu.CompilerParams(vmem_limit_bytes=60 * 1024 * 1024),
        name="arrange",
    )(incoming)


def solution(mesh):
    placed = (
        P("ctx", "rows"),
        P("ctx", None),
        P("ctx", None),
        P("rows", None),
        P("rows", None),
        P("ctx"),
    )
    return jax.shard_map(
        body, mesh=mesh, in_specs=placed, out_specs=P(("ctx", "rows"), None), check_vma=False
    )
```

```python
import functools

import jax
import jax.numpy as jnp
from jax import lax
from jax.experimental import pallas as pl
from jax.experimental.pallas import tpu as pltpu
from jax.sharding import PartitionSpec as P

HEADS = 32
KV_HEADS = 8
DH = 128
BLOCK = 128
NEG = -1e30
ROW_CEILING = 1 << 30
EMPTY = 1048576.0
SCALE2 = DH**-0.5 * 1.4426950408889634
GROUP = 4
SLOT = 32
PIECE = {(0, 0): 0, (3, 0): 1, (1, 0): 2, (0, 1): 3, (2, 0): 4, (1, 1): 5, (3, 1): 6, (2, 1): 7}
ANY = pl.BlockSpec(memory_space=pl.ANY)
SMEM = pl.BlockSpec(memory_space=pltpu.SMEM)
VMEM = pl.BlockSpec(memory_space=pltpu.VMEM)


def dot_t(a, b):
    return lax.dot_general(a, b, (((1,), (1,)), ((), ())), preferred_element_type=jnp.float32)


def own_kernel(meta, keys, values, own_ref, keys_ref, values_ref, value_s, sem):
    column = pl.ds(pl.multiple_of(meta[1] * DH, DH), DH)
    value_copy = pltpu.make_async_copy(values.at[:, column], value_s, sem.at[0])
    key_copy = pltpu.make_async_copy(keys.at[:, column], keys_ref, sem.at[1])
    value_copy.start()
    key_copy.start()
    value_copy.wait()
    for start in range(0, value_s.shape[0], BLOCK):
        rows = slice(start, start + BLOCK)
        values_ref[rows, :] = value_s[rows, :].T
    key_copy.wait()

    @pl.when(meta[0] == 0)
    def _():
        own_ref[...] = keys_ref[...]

    @pl.when(meta[0] != 0)
    def _():
        own_ref[...] = values_ref[...]


def attend_kernel(sizes, slots, heads, meta, lists, counts, sent, start, q_ref, rank_ref, *rest):
    rest = list(rest)
    take = lambda n: [rest.pop(0) for _ in range(n)]
    pieces = len(sizes)
    own, mine, other = take(2), take(pieces), take(pieces)
    out_ref, k_s, v_s = take(3)
    score_s = [take(heads), take(heads)]
    peak_s = [take(heads), take(heads)]
    att, sorted_s, sem = take(3)
    shard = q_ref.shape[0]
    nblk = shard // BLOCK
    core = meta[0]
    key_copies, value_copies = [], []
    for number, (ref, to, held) in enumerate(zip(own, (k_s, v_s), (key_copies, value_copies))):
        copy = pltpu.make_async_copy(ref, to.at[pl.ds(0, shard)], sem.at[number])
        copy.start()
        held.append(copy)
    begin = shard
    for p in range(pieces):
        spot = pl.ds(begin, sizes[p])
        begin += sizes[p]
        number = 2 + 2 * p

        @pl.when(core == 0)
        def _():
            pltpu.make_async_copy(mine[p], k_s.at[spot], sem.at[number]).start()
            pltpu.make_async_copy(other[p], v_s.at[spot], sem.at[number + 1]).start()

        @pl.when(core != 0)
        def _():
            pltpu.make_async_copy(other[p], k_s.at[spot], sem.at[number]).start()
            pltpu.make_async_copy(mine[p], v_s.at[spot], sem.at[number + 1]).start()

        key_copies.append(pltpu.make_async_copy(mine[p], k_s.at[spot], sem.at[number]))
        value_copies.append(pltpu.make_async_copy(mine[p], v_s.at[spot], sem.at[number + 1]))

    def block_of(ref, index):
        return ref[pl.ds(pl.multiple_of(index * BLOCK, BLOCK), BLOCK), :]

    def lane_of(h):
        return slice(h * DH, (h + 1) * DH)

    chunks = [[-1]] + [list(range(c, min(c + GROUP, slots))) for c in range(0, slots, GROUP)]

    def place(slot):
        return slice((slot + 1) * BLOCK, (slot + 2) * BLOCK)

    def fold(op, reduced, parts):
        return functools.reduce(op, [reduced(p.reshape(-1, 8, BLOCK), axis=0) for p in parts])

    def score(qb, h, turn, group, peaks):
        row = h * nblk + qb
        query = block_of(q_ref, qb)[:, lane_of(h)]
        if group == [-1]:
            tri = lax.broadcasted_iota(jnp.int32, (BLOCK, BLOCK), 0) <= lax.broadcasted_iota(
                jnp.int32, (BLOCK, BLOCK), 1
            )
            parts = [jnp.where(tri, dot_t(block_of(k_s, qb), query), NEG)]
        else:
            keys_block = jnp.concatenate([block_of(k_s, lists[row, u]) for u in group], axis=0)
            scores = dot_t(keys_block, query)
            parts = [
                jnp.where(u < counts[row], scores[i * BLOCK : (i + 1) * BLOCK], NEG) for i, u in enumerate(group)
            ]
        for u, one in zip(group, parts):
            score_s[turn][h][place(u), :] = one
        peaks[h] = fold(jnp.maximum, jnp.max, parts + ([peaks[h]] if h in peaks else []))
        if group == chunks[-1]:
            peak_s[turn][h][...] = peaks[h]

    def mix(qb, h, turn, group, state):
        high, total, mixed = state
        row = h * nblk + qb
        weights = [jnp.exp2((score_s[turn][h][place(u), :] - high) * SCALE2) for u in group]
        low = jnp.concatenate([w.astype(jnp.bfloat16) for w in weights], axis=0)
        values_block = jnp.concatenate([block_of(v_s, qb if u < 0 else lists[row, u]) for u in group], axis=1)
        fresh = jnp.dot(values_block, low, preferred_element_type=jnp.float32)
        total = fold(jnp.add, jnp.sum, weights + ([] if total is None else [total]))
        return high, total, fresh if mixed is None else mixed + fresh

    def phase(qb, turn, ahead):
        if qb is not None:
            states = [(jnp.max(peak_s[turn][h][...], axis=0, keepdims=True), None, None) for h in range(heads)]
        peaks = {}
        for group in chunks:
            for h in range(heads):
                score(ahead, h, 1 - turn, group, peaks)
            if qb is not None:
                for h in range(heads):
                    states[h] = mix(qb, h, turn, group, states[h])
        if qb is not None:
            for h in range(heads):
                _, total, mixed = states[h]
                attended = mixed / jnp.sum(total, axis=0, keepdims=True)
                rows = pl.ds(pl.multiple_of((qb * heads + h) * DH, DH), DH)
                att[rows, :] = attended.astype(jnp.bfloat16)

    for copy in key_copies:
        copy.wait()

    def lead(qb, _):
        phase(None, 1, qb)
        return 0

    lax.fori_loop(0, jnp.minimum(counts[0], 0) + 1, lead, 0)
    for copy in value_copies:
        copy.wait()

    def two_blocks(pair, _):
        qb = 2 * pair
        phase(qb, 0, qb + 1)
        phase(qb + 1, 1, jnp.minimum(qb + 2, nblk - 1))
        return 0

    lax.fori_loop(0, nblk // 2, two_blocks, 0)
    scatter_rows(sent, start, rank_ref, att, sorted_s, out_ref)


def scatter_rows(sent, start, rank_ref, att, sorted_s, out_ref):
    shard = rank_ref.shape[1]
    nblk = shard // BLOCK
    width = att.shape[0] // nblk
    owners = sent.shape[0]
    batch = 512

    def per_batch(step, _):
        place = lax.broadcasted_iota(jnp.int32, (batch, shard), 0)
        hot = jnp.where(rank_ref[...] - step * batch == place, 1.0, 0.0).astype(jnp.bfloat16)
        rows = pl.ds(pl.multiple_of(step * batch, batch), batch)
        sorted_s[rows, :] = dot_t(hot, jnp.concatenate([att[i * width : (i + 1) * width, :] for i in range(nblk)], axis=1))
        return 0

    lax.fori_loop(0, shard // batch, per_batch, 0)
    sorted_s[shard:, :] = jnp.zeros((SLOT + 8, width), jnp.float32)

    def per_owners(step, _):
        line = lax.broadcasted_iota(jnp.int32, (SLOT, width), 0)
        for u in range(8):
            owner = step * 8 + u
            shift = lax.rem(start[owner], 8)
            rows = sorted_s[pl.ds(pl.multiple_of(start[owner] - shift, 8), SLOT + 8), :]
            rows = pltpu.roll(rows, SLOT + 8 - shift, 0)[:SLOT]
            kept = jnp.where(line < sent[owner], rows, EMPTY).astype(jnp.bfloat16)
            out_ref[pl.ds(pl.multiple_of(owner * SLOT, SLOT), SLOT), :] = kept
        return 0

    lax.fori_loop(0, owners // 8, per_owners, 0)


def arrange_kernel(in_ref, out_ref):
    shards, groups, capacity, width = in_ref.shape
    slots = shards * capacity
    rows = out_ref.shape[0]
    block = in_ref[:, 0].reshape(slots, width)
    used = jnp.where(block[:, :rows].astype(jnp.float32) < EMPTY / 2, 1.0, 0.0).astype(jnp.bfloat16)
    one = lax.broadcasted_iota(jnp.int32, (slots, slots), 0)
    two = lax.broadcasted_iota(jnp.int32, (slots, slots), 1)
    contract = (((0,), (0,)), ((), ()))
    before = lax.dot_general(
        used, jnp.where(one < two, 1.0, 0.0).astype(jnp.bfloat16), contract, preferred_element_type=jnp.float32
    )
    here = lax.dot_general(
        used, jnp.where(one == two, 1.0, 0.0).astype(jnp.bfloat16), contract, preferred_element_type=jnp.float32
    )
    line = lax.broadcasted_iota(jnp.int32, (rows, slots), 0).astype(jnp.float32)
    pick = jnp.where((before == line) & (here > 0.5), 1.0, 0.0).astype(jnp.bfloat16)
    for g in range(groups):
        block = in_ref[:, g].reshape(slots, width)
        out_ref[:, g * width : (g + 1) * width] = jnp.dot(pick, block, preferred_element_type=jnp.float32).astype(
            jnp.bfloat16
        )


def block_lists(verticals, slashes, place, nblk, nshards):
    heads = verticals.shape[0]
    query_blocks = place * nblk + jnp.arange(nblk, dtype=jnp.int32)
    vertical = jnp.broadcast_to(verticals[:, None, :], (heads, nblk, verticals.shape[1]))
    slash = query_blocks[None, :, None] - slashes[:, None, :]
    cand = jnp.concatenate([vertical, slash], axis=2)
    slots = cand.shape[2]
    order = jnp.arange(slots, dtype=jnp.int32)
    earlier = order[None, :] < order[:, None]
    repeated = jnp.any((cand[:, :, :, None] == cand[:, :, None, :]) & earlier[None, None], axis=3)
    valid = (cand >= 0) & (cand < query_blocks[None, :, None]) & jnp.logical_not(repeated)
    source = cand // nblk
    dx = (source // 2 - place // 2) % (nshards // 2)
    dz = (source - place) % 2
    piece = jnp.zeros_like(cand)
    for (ox, oz), number in PIECE.items():
        piece = jnp.where((dx == ox) & (dz == oz), number, piece)
    local = jnp.clip(piece * nblk + cand % nblk, 0, nshards * nblk - 1)
    rank = jnp.sum((valid[:, :, None, :] & earlier[None, None]).astype(jnp.int32), axis=3)
    chosen = valid[:, :, :, None] & (rank[:, :, :, None] == order)
    lists = jnp.sum(jnp.where(chosen, local[:, :, :, None], 0), axis=2)
    return lists.reshape(heads * nblk, slots), jnp.sum(valid.astype(jnp.int32), axis=2).reshape(heads * nblk)


def body(queries, keys, values, verticals, slashes, destination):
    cycle = lax.axis_size("ctx")
    groups = lax.axis_size("rows")
    place = lax.axis_index("ctx")
    group = lax.axis_index("rows")
    rows_here = queries.shape[0]
    heads = verticals.shape[0]
    nblk = rows_here // BLOCK
    devices = cycle * groups
    own_rows = rows_here // groups
    kv_index = group * heads // (HEADS // KV_HEADS)
    core = group % 2

    meta = jnp.stack([core, kv_index]).astype(jnp.int32)
    own, *here = pl.pallas_call(
        own_kernel,
        out_shape=[jax.ShapeDtypeStruct((rows_here, DH), jnp.bfloat16)] * 3,
        in_specs=[SMEM, ANY, ANY],
        out_specs=[VMEM] * 3,
        scratch_shapes=[pltpu.VMEM((rows_here, DH), jnp.bfloat16), pltpu.SemaphoreType.DMA((2,))],
        compiler_params=pltpu.CompilerParams(vmem_limit_bytes=24 * 1024 * 1024),
        name="own",
    )(meta, keys, values)

    def along_x(x, step):
        return lax.ppermute(x, "ctx", [(c, (c + 2 * step) % cycle) for c in range(cycle)])

    def along_z(x):
        return lax.ppermute(x, "ctx", [(c, c ^ 1) for c in range(cycle)])

    def swap(x):
        return lax.ppermute(x, "rows", [(r, r ^ 1) for r in range(groups)])

    half = rows_here // 2
    p1 = along_x(own, 1)
    p2 = along_x(own, -1)
    p3 = along_z(own)

    lists, counts = block_lists(verticals, slashes, place, nblk, cycle)
    owner = destination // own_rows
    member = owner[:, None] == jnp.arange(devices, dtype=jnp.int32)[None, :]
    first_row = jnp.min(jnp.where(member, destination[:, None], ROW_CEILING), axis=0)
    sent = jnp.sum(member.astype(jnp.int32), axis=0)
    numbers = jnp.arange(devices, dtype=jnp.int32)
    start = jnp.sum(jnp.where(numbers[:, None] < numbers[None, :], sent[:, None], 0), axis=0)
    rank = destination + jnp.sum(jnp.where(member, (start - first_row)[None, :], 0), axis=1)
    small = (lists, counts, sent, start, rank.reshape(1, rows_here))
    p1, p3, small = lax.optimization_barrier((p1, p3, small))

    p4 = along_x(p1, 1)
    p5 = along_x(p3, -1)
    p6 = along_z(p1)
    mine = [jnp.concatenate([p1, p2, p3], axis=0)]
    other = [swap(mine[0])]
    p7 = along_x(p6[:half], 1)
    p8 = along_x(p5[half:], -1)
    mine += [jnp.concatenate([p4, p5, p6], axis=0), p7, p8]
    other += [swap(x) for x in mine[1:]]

    lists, counts, sent, start, rank = small
    slots = lists.shape[1]
    outgoing = pl.pallas_call(
        functools.partial(attend_kernel, [x.shape[0] for x in mine], slots, heads),
        out_shape=jax.ShapeDtypeStruct((devices * SLOT, heads * DH), jnp.bfloat16),
        in_specs=[SMEM] * 5 + [VMEM] * 2 + [ANY] * (2 + 2 * len(mine)),
        out_specs=VMEM,
        scratch_shapes=[pltpu.VMEM((cycle * rows_here, DH), jnp.bfloat16)] * 2
        + [pltpu.VMEM(((slots + 1) * BLOCK, BLOCK), jnp.float32)] * (2 * heads)
        + [pltpu.VMEM((8, BLOCK), jnp.float32)] * (2 * heads)
        + [
            pltpu.VMEM((nblk * heads * DH, BLOCK), jnp.bfloat16),
            pltpu.VMEM((rows_here + SLOT + 8, heads * DH), jnp.float32),
            pltpu.SemaphoreType.DMA((2 + 2 * len(mine),)),
        ],
        compiler_params=pltpu.CompilerParams(vmem_limit_bytes=28 * 1024 * 1024),
        name="attend",
    )(meta, lists, counts, sent, start, queries, rank, *here, *mine, *other)

    incoming = lax.all_to_all(
        outgoing.reshape(devices, SLOT, heads * DH), ("ctx", "rows"), split_axis=0, concat_axis=0, tiled=True
    )
    incoming = incoming.reshape(cycle, groups, SLOT, heads * DH)
    return pl.pallas_call(
        arrange_kernel,
        out_shape=jax.ShapeDtypeStruct((own_rows, groups * heads * DH), jnp.bfloat16),
        in_specs=[VMEM],
        out_specs=VMEM,
        compiler_params=pltpu.CompilerParams(vmem_limit_bytes=28 * 1024 * 1024),
        name="arrange",
    )(incoming)


def solution(mesh):
    placed = (
        P("ctx", "rows"),
        P("ctx", None),
        P("ctx", None),
        P("rows", None),
        P("rows", None),
        P("ctx"),
    )
    return jax.shard_map(
        body, mesh=mesh, in_specs=placed, out_specs=P(("ctx", "rows"), None), check_vma=False
    )
```

```python
import functools

import jax
import jax.numpy as jnp
from jax import lax
from jax.experimental import pallas as pl
from jax.experimental.pallas import tpu as pltpu
from jax.sharding import PartitionSpec as P

HEADS = 32
KV_HEADS = 8
DH = 128
BLOCK = 128
NEG = -1e30
ROW_CEILING = 1 << 30
EMPTY = 1048576.0
SCALE2 = DH**-0.5 * 1.4426950408889634
GROUP = 4
SLOT = 32
PIECE = {(0, 0): 0, (3, 0): 1, (1, 0): 2, (0, 1): 3, (2, 0): 4, (1, 1): 5, (3, 1): 6, (2, 1): 7}
ANY = pl.BlockSpec(memory_space=pl.ANY)
HBM = pl.BlockSpec(memory_space=pltpu.HBM)
SMEM = pl.BlockSpec(memory_space=pltpu.SMEM)
VMEM = pl.BlockSpec(memory_space=pltpu.VMEM)


def dot_t(a, b):
    return lax.dot_general(a, b, (((1,), (1,)), ((), ())), preferred_element_type=jnp.float32)


def own_kernel(meta, keys, values, own_ref, keys_ref, values_ref, value_s, sem):
    column = pl.ds(pl.multiple_of(meta[1] * DH, DH), DH)
    value_copy = pltpu.make_async_copy(values.at[:, column], value_s, sem.at[0])
    key_copy = pltpu.make_async_copy(keys.at[:, column], keys_ref, sem.at[1])
    value_copy.start()
    key_copy.start()
    value_copy.wait()
    for start in range(0, value_s.shape[0], BLOCK):
        rows = slice(start, start + BLOCK)
        values_ref[rows, :] = value_s[rows, :].T
    key_copy.wait()

    @pl.when(meta[0] == 0)
    def _():
        own_ref[...] = keys_ref[...]

    @pl.when(meta[0] != 0)
    def _():
        own_ref[...] = values_ref[...]


def attend_kernel(sizes, slots, heads, meta, lists, counts, sent, start, q_ref, rank_ref, *rest):
    rest = list(rest)
    take = lambda n: [rest.pop(0) for _ in range(n)]
    pieces = len(sizes)
    own, mine, other = take(2), take(pieces), take(pieces)
    out_ref, k_s, v_s = take(3)
    score_s = [take(heads), take(heads)]
    peak_s = [take(heads), take(heads)]
    att, sorted_s, sem = take(3)
    shard = q_ref.shape[0]
    nblk = shard // BLOCK
    core = meta[0]
    key_copies, value_copies = [], []
    for number, (ref, to, held) in enumerate(zip(own, (k_s, v_s), (key_copies, value_copies))):
        copy = pltpu.make_async_copy(ref, to.at[pl.ds(0, shard)], sem.at[number])
        copy.start()
        held.append(copy)
    begin = shard
    for p in range(pieces):
        spot = pl.ds(begin, sizes[p])
        begin += sizes[p]
        number = 2 + 2 * p

        @pl.when(core == 0)
        def _():
            pltpu.make_async_copy(mine[p], k_s.at[spot], sem.at[number]).start()
            pltpu.make_async_copy(other[p], v_s.at[spot], sem.at[number + 1]).start()

        @pl.when(core != 0)
        def _():
            pltpu.make_async_copy(other[p], k_s.at[spot], sem.at[number]).start()
            pltpu.make_async_copy(mine[p], v_s.at[spot], sem.at[number + 1]).start()

        key_copies.append(pltpu.make_async_copy(mine[p], k_s.at[spot], sem.at[number]))
        value_copies.append(pltpu.make_async_copy(mine[p], v_s.at[spot], sem.at[number + 1]))

    def block_of(ref, index):
        return ref[pl.ds(pl.multiple_of(index * BLOCK, BLOCK), BLOCK), :]

    def lane_of(h):
        return slice(h * DH, (h + 1) * DH)

    chunks = [[-1]] + [list(range(c, min(c + GROUP, slots))) for c in range(0, slots, GROUP)]

    def place(slot):
        return slice((slot + 1) * BLOCK, (slot + 2) * BLOCK)

    def fold(reduced, block):
        return reduced(block.reshape(-1, 8, BLOCK), axis=0)

    def score(qb, h, turn, group, peaks):
        row = h * nblk + qb
        query = block_of(q_ref, qb)[:, lane_of(h)]
        if group == [-1]:
            tri = lax.broadcasted_iota(jnp.int32, (BLOCK, BLOCK), 0) <= lax.broadcasted_iota(
                jnp.int32, (BLOCK, BLOCK), 1
            )
            parts = [jnp.where(tri, dot_t(block_of(k_s, qb), query), NEG)]
        else:
            keys_block = jnp.concatenate([block_of(k_s, lists[row, u]) for u in group], axis=0)
            scores = dot_t(keys_block, query)
            parts = [scores[i * BLOCK : (i + 1) * BLOCK] for i in range(len(group))]
        for u, one in zip(group, parts):
            score_s[turn][h][place(u), :] = one
            peak = jnp.where(u < counts[row], fold(jnp.max, one), NEG)
            peaks[h] = jnp.maximum(peaks[h], peak) if h in peaks else peak
        if group == chunks[-1]:
            peak_s[turn][h][...] = peaks[h]

    def mix(qb, h, turn, group, state):
        high, total, mixed = state
        row = h * nblk + qb
        tops = [jnp.where(u < counts[row], high, -NEG) for u in group]
        weights = [jnp.exp2((score_s[turn][h][place(u), :] - top) * SCALE2) for u, top in zip(group, tops)]
        low = jnp.concatenate([w.astype(jnp.bfloat16) for w in weights], axis=0)
        values_block = jnp.concatenate([block_of(v_s, qb if u < 0 else lists[row, u]) for u in group], axis=1)
        fresh = jnp.dot(values_block, low, preferred_element_type=jnp.float32)
        for w in weights:
            total = fold(jnp.sum, w) if total is None else total + fold(jnp.sum, w)
        return high, total, fresh if mixed is None else mixed + fresh

    def phase(qb, turn, ahead):
        if qb is not None:
            states = [(jnp.max(peak_s[turn][h][...], axis=0, keepdims=True), None, None) for h in range(heads)]
        peaks = {}
        for group in chunks:
            for h in range(heads):
                score(ahead, h, 1 - turn, group, peaks)
            if qb is not None:
                for h in range(heads):
                    states[h] = mix(qb, h, turn, group, states[h])
        if qb is not None:
            for h in range(heads):
                _, total, mixed = states[h]
                attended = mixed / jnp.sum(total, axis=0, keepdims=True)
                rows = pl.ds(pl.multiple_of((qb * heads + h) * DH, DH), DH)
                att[rows, :] = attended.astype(jnp.bfloat16)

    for copy in key_copies:
        copy.wait()

    def lead(qb, _):
        phase(None, 1, qb)
        return 0

    lax.fori_loop(0, jnp.minimum(counts[0], 0) + 1, lead, 0)
    for copy in value_copies:
        copy.wait()

    def two_blocks(pair, _):
        qb = 2 * pair
        phase(qb, 0, qb + 1)
        phase(qb + 1, 1, jnp.minimum(qb + 2, nblk - 1))
        return 0

    lax.fori_loop(0, nblk // 2, two_blocks, 0)
    scatter_rows(sent, start, rank_ref, att, sorted_s, out_ref)


def scatter_rows(sent, start, rank_ref, att, sorted_s, out_ref):
    shard = rank_ref.shape[1]
    nblk = shard // BLOCK
    width = att.shape[0] // nblk
    owners = sent.shape[0]
    batch = 512

    def per_batch(step, _):
        place = lax.broadcasted_iota(jnp.int32, (batch, shard), 0)
        hot = jnp.where(rank_ref[...] - step * batch == place, 1.0, 0.0).astype(jnp.bfloat16)
        rows = pl.ds(pl.multiple_of(step * batch, batch), batch)
        sorted_s[rows, :] = dot_t(hot, jnp.concatenate([att[i * width : (i + 1) * width, :] for i in range(nblk)], axis=1))
        return 0

    lax.fori_loop(0, shard // batch, per_batch, 0)
    sorted_s[shard:, :] = jnp.zeros((SLOT + 8, width), jnp.float32)

    def per_owners(step, _):
        line = lax.broadcasted_iota(jnp.int32, (SLOT, width), 0)
        for u in range(8):
            owner = step * 8 + u
            shift = lax.rem(start[owner], 8)
            rows = sorted_s[pl.ds(pl.multiple_of(start[owner] - shift, 8), SLOT + 8), :]
            rows = pltpu.roll(rows, SLOT + 8 - shift, 0)[:SLOT]
            kept = jnp.where(line < sent[owner], rows, EMPTY).astype(jnp.bfloat16)
            out_ref[pl.ds(pl.multiple_of(owner * SLOT, SLOT), SLOT), :] = kept
        return 0

    lax.fori_loop(0, owners // 8, per_owners, 0)


def arrange_kernel(in_ref, out_ref):
    shards, groups, capacity, width = in_ref.shape
    slots = shards * capacity
    rows = out_ref.shape[0]
    block = in_ref[:, 0].reshape(slots, width)
    used = jnp.where(block[:, :rows].astype(jnp.float32) < EMPTY / 2, 1.0, 0.0).astype(jnp.bfloat16)
    one = lax.broadcasted_iota(jnp.int32, (slots, slots), 0)
    two = lax.broadcasted_iota(jnp.int32, (slots, slots), 1)
    contract = (((0,), (0,)), ((), ()))
    before = lax.dot_general(
        used, jnp.where(one < two, 1.0, 0.0).astype(jnp.bfloat16), contract, preferred_element_type=jnp.float32
    )
    here = lax.dot_general(
        used, jnp.where(one == two, 1.0, 0.0).astype(jnp.bfloat16), contract, preferred_element_type=jnp.float32
    )
    line = lax.broadcasted_iota(jnp.int32, (rows, slots), 0).astype(jnp.float32)
    pick = jnp.where((before == line) & (here > 0.5), 1.0, 0.0).astype(jnp.bfloat16)
    for g in range(groups):
        block = in_ref[:, g].reshape(slots, width)
        out_ref[:, g * width : (g + 1) * width] = jnp.dot(pick, block, preferred_element_type=jnp.float32).astype(
            jnp.bfloat16
        )


def block_lists(verticals, slashes, place, nblk, nshards):
    heads = verticals.shape[0]
    query_blocks = place * nblk + jnp.arange(nblk, dtype=jnp.int32)
    vertical = jnp.broadcast_to(verticals[:, None, :], (heads, nblk, verticals.shape[1]))
    slash = query_blocks[None, :, None] - slashes[:, None, :]
    cand = jnp.concatenate([vertical, slash], axis=2)
    slots = cand.shape[2]
    order = jnp.arange(slots, dtype=jnp.int32)
    earlier = order[None, :] < order[:, None]
    repeated = jnp.any((cand[:, :, :, None] == cand[:, :, None, :]) & earlier[None, None], axis=3)
    valid = (cand >= 0) & (cand < query_blocks[None, :, None]) & jnp.logical_not(repeated)
    source = cand // nblk
    dx = (source // 2 - place // 2) % (nshards // 2)
    dz = (source - place) % 2
    piece = jnp.zeros_like(cand)
    for (ox, oz), number in PIECE.items():
        piece = jnp.where((dx == ox) & (dz == oz), number, piece)
    local = jnp.clip(piece * nblk + cand % nblk, 0, nshards * nblk - 1)
    rank = jnp.sum((valid[:, :, None, :] & earlier[None, None]).astype(jnp.int32), axis=3)
    chosen = valid[:, :, :, None] & (rank[:, :, :, None] == order)
    lists = jnp.sum(jnp.where(chosen, local[:, :, :, None], 0), axis=2)
    return lists.reshape(heads * nblk, slots), jnp.sum(valid.astype(jnp.int32), axis=2).reshape(heads * nblk)


def body(queries, keys, values, verticals, slashes, destination):
    cycle = lax.axis_size("ctx")
    groups = lax.axis_size("rows")
    place = lax.axis_index("ctx")
    group = lax.axis_index("rows")
    rows_here = queries.shape[0]
    heads = verticals.shape[0]
    nblk = rows_here // BLOCK
    devices = cycle * groups
    own_rows = rows_here // groups
    kv_index = group * heads // (HEADS // KV_HEADS)
    core = group % 2

    meta = jnp.stack([core, kv_index]).astype(jnp.int32)
    own, *here = pl.pallas_call(
        own_kernel,
        out_shape=[jax.ShapeDtypeStruct((rows_here, DH), jnp.bfloat16)] * 3,
        in_specs=[SMEM, HBM, HBM],
        out_specs=[VMEM] * 3,
        scratch_shapes=[pltpu.VMEM((rows_here, DH), jnp.bfloat16), pltpu.SemaphoreType.DMA((2,))],
        compiler_params=pltpu.CompilerParams(vmem_limit_bytes=24 * 1024 * 1024),
        name="own",
    )(meta, keys, values)

    def along_x(x, step):
        return lax.ppermute(x, "ctx", [(c, (c + 2 * step) % cycle) for c in range(cycle)])

    def along_z(x):
        return lax.ppermute(x, "ctx", [(c, c ^ 1) for c in range(cycle)])

    def swap(x):
        return lax.ppermute(x, "rows", [(r, r ^ 1) for r in range(groups)])

    half = rows_here // 2
    p1 = along_x(own, 1)
    p3 = along_z(own)
    p2 = along_x(own, -1)

    lists, counts = block_lists(verticals, slashes, place, nblk, cycle)
    owner = destination // own_rows
    member = owner[:, None] == jnp.arange(devices, dtype=jnp.int32)[None, :]
    first_row = jnp.min(jnp.where(member, destination[:, None], ROW_CEILING), axis=0)
    sent = jnp.sum(member.astype(jnp.int32), axis=0)
    numbers = jnp.arange(devices, dtype=jnp.int32)
    start = jnp.sum(jnp.where(numbers[:, None] < numbers[None, :], sent[:, None], 0), axis=0)
    rank = destination + jnp.sum(jnp.where(member, (start - first_row)[None, :], 0), axis=1)
    small = (lists, counts, sent, start, rank.reshape(1, rows_here))
    p1, p3, small = lax.optimization_barrier((p1, p3, small))

    p6a, p5b = along_z(p1[:half]), along_x(p3[half:], -1)
    p4 = along_x(p1, 1)
    p6b, p5a = along_z(p1[half:]), along_x(p3[:half], -1)
    mine = [jnp.concatenate([p1, p2, p3], axis=0)]
    other = [swap(mine[0])]
    p7 = along_x(p6a, 1)
    p8 = along_x(p5b, -1)
    mine += [jnp.concatenate([p4, p5a, p5b, p6a, p6b], axis=0), p7, p8]
    other += [swap(x) for x in mine[1:]]

    lists, counts, sent, start, rank = small
    slots = lists.shape[1]
    outgoing = pl.pallas_call(
        functools.partial(attend_kernel, [x.shape[0] for x in mine], slots, heads),
        out_shape=jax.ShapeDtypeStruct((devices * SLOT, heads * DH), jnp.bfloat16),
        in_specs=[SMEM] * 5 + [VMEM] * 2 + [ANY] * (2 + 2 * len(mine)),
        out_specs=VMEM,
        scratch_shapes=[pltpu.VMEM((cycle * rows_here, DH), jnp.bfloat16)] * 2
        + [pltpu.VMEM(((slots + 1) * BLOCK, BLOCK), jnp.float32)] * (2 * heads)
        + [pltpu.VMEM((8, BLOCK), jnp.float32)] * (2 * heads)
        + [
            pltpu.VMEM((nblk * heads * DH, BLOCK), jnp.bfloat16),
            pltpu.VMEM((rows_here + SLOT + 8, heads * DH), jnp.float32),
            pltpu.SemaphoreType.DMA((2 + 2 * len(mine),)),
        ],
        compiler_params=pltpu.CompilerParams(vmem_limit_bytes=28 * 1024 * 1024),
        name="attend",
    )(meta, lists, counts, sent, start, queries, rank, *here, *mine, *other)

    incoming = lax.all_to_all(
        outgoing.reshape(devices, SLOT, heads * DH), ("ctx", "rows"), split_axis=0, concat_axis=0, tiled=True
    )
    incoming = incoming.reshape(cycle, groups, SLOT, heads * DH)
    return pl.pallas_call(
        arrange_kernel,
        out_shape=jax.ShapeDtypeStruct((own_rows, groups * heads * DH), jnp.bfloat16),
        in_specs=[VMEM],
        out_specs=VMEM,
        compiler_params=pltpu.CompilerParams(vmem_limit_bytes=28 * 1024 * 1024),
        name="arrange",
    )(incoming)


def solution(mesh):
    placed = (
        P("ctx", "rows"),
        P("ctx", None),
        P("ctx", None),
        P("rows", None),
        P("rows", None),
        P("ctx"),
    )
    return jax.shard_map(
        body, mesh=mesh, in_specs=placed, out_specs=P(("ctx", "rows"), None), check_vma=False
    )
```

```python
import functools

import jax
import jax.numpy as jnp
from jax import lax
from jax.experimental import pallas as pl
from jax.experimental.pallas import tpu as pltpu
from jax.sharding import PartitionSpec as P

HEADS = 32
KV_HEADS = 8
DH = 128
BLOCK = 128
NEG = -1e30
ROW_CEILING = 1 << 30
EMPTY = 1048576.0
SCALE2 = DH**-0.5 * 1.4426950408889634
GROUP = 4
SLOT = 32
PIECE = {(0, 0): 0, (3, 0): 1, (1, 0): 2, (0, 1): 3, (2, 0): 4, (1, 1): 5, (3, 1): 6, (2, 1): 7}
ANY = pl.BlockSpec(memory_space=pl.ANY)
SMEM = pl.BlockSpec(memory_space=pltpu.SMEM)
VMEM = pl.BlockSpec(memory_space=pltpu.VMEM)


def dot_t(a, b):
    return lax.dot_general(a, b, (((1,), (1,)), ((), ())), preferred_element_type=jnp.float32)


def own_kernel(meta, keys, values, own_ref, keys_ref, values_ref, value_s, sem):
    column = pl.ds(pl.multiple_of(meta[1] * DH, DH), DH)
    value_copy = pltpu.make_async_copy(values.at[:, column], value_s, sem.at[0])
    key_copy = pltpu.make_async_copy(keys.at[:, column], keys_ref, sem.at[1])
    value_copy.start()
    key_copy.start()
    value_copy.wait()
    for start in range(0, value_s.shape[0], BLOCK):
        rows = slice(start, start + BLOCK)
        values_ref[rows, :] = value_s[rows, :].T
    key_copy.wait()

    @pl.when(meta[0] == 0)
    def _():
        own_ref[...] = keys_ref[...]

    @pl.when(meta[0] != 0)
    def _():
        own_ref[...] = values_ref[...]


def attend_kernel(sizes, slots, heads, meta, lists, counts, sent, start, q_ref, rank_ref, *rest):
    rest = list(rest)
    take = lambda n: [rest.pop(0) for _ in range(n)]
    pieces = len(sizes)
    own, mine, other = take(2), take(pieces), take(pieces)
    out_ref, k_s, v_s = take(3)
    score_s = [take(heads), take(heads)]
    peak_s = [take(heads), take(heads)]
    att, sorted_s, sem = take(3)
    shard = q_ref.shape[0]
    nblk = shard // BLOCK
    core = meta[0]
    key_copies, value_copies = [], []
    for number, (ref, to, held) in enumerate(zip(own, (k_s, v_s), (key_copies, value_copies))):
        copy = pltpu.make_async_copy(ref, to.at[pl.ds(0, shard)], sem.at[number])
        copy.start()
        held.append(copy)
    begin = shard
    for p in range(pieces):
        spot = pl.ds(begin, sizes[p])
        begin += sizes[p]
        number = 2 + 2 * p

        @pl.when(core == 0)
        def _():
            pltpu.make_async_copy(mine[p], k_s.at[spot], sem.at[number]).start()
            pltpu.make_async_copy(other[p], v_s.at[spot], sem.at[number + 1]).start()

        @pl.when(core != 0)
        def _():
            pltpu.make_async_copy(other[p], k_s.at[spot], sem.at[number]).start()
            pltpu.make_async_copy(mine[p], v_s.at[spot], sem.at[number + 1]).start()

        key_copies.append(pltpu.make_async_copy(mine[p], k_s.at[spot], sem.at[number]))
        value_copies.append(pltpu.make_async_copy(mine[p], v_s.at[spot], sem.at[number + 1]))

    def block_of(ref, index):
        return ref[pl.ds(pl.multiple_of(index * BLOCK, BLOCK), BLOCK), :]

    def lane_of(h):
        return slice(h * DH, (h + 1) * DH)

    chunks = [[-1]] + [list(range(c, min(c + GROUP, slots))) for c in range(0, slots, GROUP)]

    def place(slot):
        return slice((slot + 1) * BLOCK, (slot + 2) * BLOCK)

    def fold(reduced, block):
        return reduced(block.reshape(-1, 8, BLOCK), axis=0)

    def score(qb, h, turn, group, peaks):
        row = h * nblk + qb
        query = block_of(q_ref, qb)[:, lane_of(h)]
        if group == [-1]:
            tri = lax.broadcasted_iota(jnp.int32, (BLOCK, BLOCK), 0) <= lax.broadcasted_iota(
                jnp.int32, (BLOCK, BLOCK), 1
            )
            parts = [jnp.where(tri, dot_t(block_of(k_s, qb), query), NEG)]
        else:
            keys_block = jnp.concatenate([block_of(k_s, lists[row, u]) for u in group], axis=0)
            scores = dot_t(keys_block, query)
            parts = [scores[i * BLOCK : (i + 1) * BLOCK] for i in range(len(group))]
        for u, one in zip(group, parts):
            score_s[turn][h][place(u), :] = one
            peak = jnp.where(u < counts[row], fold(jnp.max, one), NEG)
            peaks[h] = jnp.maximum(peaks[h], peak) if h in peaks else peak
        if group == chunks[-1]:
            peak_s[turn][h][...] = peaks[h]

    def mix(qb, h, turn, group, state):
        high, total, mixed = state
        row = h * nblk + qb
        tops = [jnp.where(u < counts[row], high, -NEG) for u in group]
        weights = [jnp.exp2((score_s[turn][h][place(u), :] - top) * SCALE2) for u, top in zip(group, tops)]
        low = jnp.concatenate([w.astype(jnp.bfloat16) for w in weights], axis=0)
        values_block = jnp.concatenate([block_of(v_s, qb if u < 0 else lists[row, u]) for u in group], axis=1)
        fresh = jnp.dot(values_block, low, preferred_element_type=jnp.float32)
        for w in weights:
            total = fold(jnp.sum, w) if total is None else total + fold(jnp.sum, w)
        return high, total, fresh if mixed is None else mixed + fresh

    def phase(qb, turn, ahead):
        if qb is not None:
            states = [(jnp.max(peak_s[turn][h][...], axis=0, keepdims=True), None, None) for h in range(heads)]
        peaks = {}
        for group in chunks:
            for h in range(heads):
                score(ahead, h, 1 - turn, group, peaks)
            if qb is not None:
                for h in range(heads):
                    states[h] = mix(qb, h, turn, group, states[h])
        if qb is not None:
            for h in range(heads):
                _, total, mixed = states[h]
                attended = mixed / jnp.sum(total, axis=0, keepdims=True)
                rows = pl.ds(pl.multiple_of((qb * heads + h) * DH, DH), DH)
                att[rows, :] = attended.astype(jnp.bfloat16)

    for copy in key_copies:
        copy.wait()

    def lead(qb, _):
        phase(None, 1, qb)
        return 0

    lax.fori_loop(0, jnp.minimum(counts[0], 0) + 1, lead, 0)
    for copy in value_copies:
        copy.wait()

    def two_blocks(pair, _):
        qb = 2 * pair
        phase(qb, 0, qb + 1)
        phase(qb + 1, 1, jnp.minimum(qb + 2, nblk - 1))
        return 0

    lax.fori_loop(0, nblk // 2, two_blocks, 0)
    scatter_rows(sent, start, rank_ref, att, sorted_s, out_ref)


def scatter_rows(sent, start, rank_ref, att, sorted_s, out_ref):
    shard = rank_ref.shape[1]
    nblk = shard // BLOCK
    width = att.shape[0] // nblk
    owners = sent.shape[0]
    batch = 512

    def per_batch(step, _):
        place = lax.broadcasted_iota(jnp.int32, (batch, shard), 0)
        hot = jnp.where(rank_ref[...] - step * batch == place, 1.0, 0.0).astype(jnp.bfloat16)
        rows = pl.ds(pl.multiple_of(step * batch, batch), batch)
        sorted_s[rows, :] = dot_t(hot, jnp.concatenate([att[i * width : (i + 1) * width, :] for i in range(nblk)], axis=1))
        return 0

    lax.fori_loop(0, shard // batch, per_batch, 0)
    sorted_s[shard:, :] = jnp.zeros((SLOT + 8, width), jnp.float32)

    def per_owners(step, _):
        line = lax.broadcasted_iota(jnp.int32, (SLOT, width), 0)
        for u in range(8):
            owner = step * 8 + u
            shift = lax.rem(start[owner], 8)
            rows = sorted_s[pl.ds(pl.multiple_of(start[owner] - shift, 8), SLOT + 8), :]
            rows = pltpu.roll(rows, SLOT + 8 - shift, 0)[:SLOT]
            kept = jnp.where(line < sent[owner], rows, EMPTY).astype(jnp.bfloat16)
            out_ref[pl.ds(pl.multiple_of(owner * SLOT, SLOT), SLOT), :] = kept
        return 0

    lax.fori_loop(0, owners // 8, per_owners, 0)


def arrange_kernel(in_ref, out_ref):
    shards, groups, capacity, width = in_ref.shape
    slots = shards * capacity
    rows = out_ref.shape[0]
    block = in_ref[:, 0].reshape(slots, width)
    used = jnp.where(block[:, :rows].astype(jnp.float32) < EMPTY / 2, 1.0, 0.0).astype(jnp.bfloat16)
    one = lax.broadcasted_iota(jnp.int32, (slots, slots), 0)
    two = lax.broadcasted_iota(jnp.int32, (slots, slots), 1)
    contract = (((0,), (0,)), ((), ()))
    before = lax.dot_general(
        used, jnp.where(one < two, 1.0, 0.0).astype(jnp.bfloat16), contract, preferred_element_type=jnp.float32
    )
    here = lax.dot_general(
        used, jnp.where(one == two, 1.0, 0.0).astype(jnp.bfloat16), contract, preferred_element_type=jnp.float32
    )
    line = lax.broadcasted_iota(jnp.int32, (rows, slots), 0).astype(jnp.float32)
    pick = jnp.where((before == line) & (here > 0.5), 1.0, 0.0).astype(jnp.bfloat16)
    for g in range(groups):
        block = in_ref[:, g].reshape(slots, width)
        out_ref[:, g * width : (g + 1) * width] = jnp.dot(pick, block, preferred_element_type=jnp.float32).astype(
            jnp.bfloat16
        )


def block_lists(verticals, slashes, place, nblk, nshards):
    heads = verticals.shape[0]
    query_blocks = place * nblk + jnp.arange(nblk, dtype=jnp.int32)
    vertical = jnp.broadcast_to(verticals[:, None, :], (heads, nblk, verticals.shape[1]))
    slash = query_blocks[None, :, None] - slashes[:, None, :]
    cand = jnp.concatenate([vertical, slash], axis=2)
    slots = cand.shape[2]
    order = jnp.arange(slots, dtype=jnp.int32)
    earlier = order[None, :] < order[:, None]
    repeated = jnp.any((cand[:, :, :, None] == cand[:, :, None, :]) & earlier[None, None], axis=3)
    valid = (cand >= 0) & (cand < query_blocks[None, :, None]) & jnp.logical_not(repeated)
    source = cand // nblk
    dx = (source // 2 - place // 2) % (nshards // 2)
    dz = (source - place) % 2
    piece = jnp.zeros_like(cand)
    for (ox, oz), number in PIECE.items():
        piece = jnp.where((dx == ox) & (dz == oz), number, piece)
    local = jnp.clip(piece * nblk + cand % nblk, 0, nshards * nblk - 1)
    rank = jnp.sum((valid[:, :, None, :] & earlier[None, None]).astype(jnp.int32), axis=3)
    chosen = valid[:, :, :, None] & (rank[:, :, :, None] == order)
    lists = jnp.sum(jnp.where(chosen, local[:, :, :, None], 0), axis=2)
    return lists.reshape(heads * nblk, slots), jnp.sum(valid.astype(jnp.int32), axis=2).reshape(heads * nblk)


def body(queries, keys, values, verticals, slashes, destination):
    cycle = lax.axis_size("ctx")
    groups = lax.axis_size("rows")
    place = lax.axis_index("ctx")
    group = lax.axis_index("rows")
    rows_here = queries.shape[0]
    heads = verticals.shape[0]
    nblk = rows_here // BLOCK
    devices = cycle * groups
    own_rows = rows_here // groups
    kv_index = group * heads // (HEADS // KV_HEADS)
    core = group % 2

    meta = jnp.stack([core, kv_index]).astype(jnp.int32)
    own, *here = pl.pallas_call(
        own_kernel,
        out_shape=[jax.ShapeDtypeStruct((rows_here, DH), jnp.bfloat16)] * 3,
        in_specs=[SMEM, ANY, ANY],
        out_specs=[VMEM] * 3,
        scratch_shapes=[pltpu.VMEM((rows_here, DH), jnp.bfloat16), pltpu.SemaphoreType.DMA((2,))],
        compiler_params=pltpu.CompilerParams(vmem_limit_bytes=60 * 1024 * 1024),
        name="own",
    )(meta, keys, values)

    def along_x(x, step):
        return lax.ppermute(x, "ctx", [(c, (c + 2 * step) % cycle) for c in range(cycle)])

    def along_z(x):
        return lax.ppermute(x, "ctx", [(c, c ^ 1) for c in range(cycle)])

    def swap(x):
        return lax.ppermute(x, "rows", [(r, r ^ 1) for r in range(groups)])

    half = rows_here // 2
    owner = destination // own_rows
    member = owner[:, None] == jnp.arange(devices, dtype=jnp.int32)[None, :]
    first_row = jnp.min(jnp.where(member, destination[:, None], ROW_CEILING), axis=0)
    sent = jnp.sum(member.astype(jnp.int32), axis=0)
    numbers = jnp.arange(devices, dtype=jnp.int32)
    start = jnp.sum(jnp.where(numbers[:, None] < numbers[None, :], sent[:, None], 0), axis=0)
    rank = destination + jnp.sum(jnp.where(member, (start - first_row)[None, :], 0), axis=1)
    p1 = along_x(own, 1)
    p3 = along_z(own)
    own, sent = lax.optimization_barrier((own, sent))
    p2 = along_x(own, -1)
    lists, counts = block_lists(verticals, slashes, place, nblk, cycle)
    small = (lists, counts, sent, start, rank.reshape(1, rows_here))
    p1, p3, small = lax.optimization_barrier((p1, p3, small))

    p4 = along_x(p1, 1)
    p5 = along_x(p3, -1)
    p6 = along_z(p1)
    mine = [jnp.concatenate([p1, p2, p3], axis=0)]
    other = [swap(mine[0])]
    p7 = along_x(p6[:half], 1)
    p8 = along_x(p5[half:], -1)
    mine += [jnp.concatenate([p4, p5, p6], axis=0), p7, p8]
    other += [swap(x) for x in mine[1:]]

    lists, counts, sent, start, rank = small
    slots = lists.shape[1]
    outgoing = pl.pallas_call(
        functools.partial(attend_kernel, [x.shape[0] for x in mine], slots, heads),
        out_shape=jax.ShapeDtypeStruct((devices * SLOT, heads * DH), jnp.bfloat16),
        in_specs=[SMEM] * 5 + [VMEM] * 2 + [ANY] * (2 + 2 * len(mine)),
        out_specs=VMEM,
        scratch_shapes=[pltpu.VMEM((cycle * rows_here, DH), jnp.bfloat16)] * 2
        + [pltpu.VMEM(((slots + 1) * BLOCK, BLOCK), jnp.float32)] * (2 * heads)
        + [pltpu.VMEM((8, BLOCK), jnp.float32)] * (2 * heads)
        + [
            pltpu.VMEM((nblk * heads * DH, BLOCK), jnp.bfloat16),
            pltpu.VMEM((rows_here + SLOT + 8, heads * DH), jnp.float32),
            pltpu.SemaphoreType.DMA((2 + 2 * len(mine),)),
        ],
        compiler_params=pltpu.CompilerParams(vmem_limit_bytes=28 * 1024 * 1024),
        name="attend",
    )(meta, lists, counts, sent, start, queries, rank, *here, *mine, *other)

    incoming = lax.all_to_all(
        outgoing.reshape(devices, SLOT, heads * DH), ("ctx", "rows"), split_axis=0, concat_axis=0, tiled=True
    )
    incoming = incoming.reshape(cycle, groups, SLOT, heads * DH)
    return pl.pallas_call(
        arrange_kernel,
        out_shape=jax.ShapeDtypeStruct((own_rows, groups * heads * DH), jnp.bfloat16),
        in_specs=[VMEM],
        out_specs=VMEM,
        compiler_params=pltpu.CompilerParams(vmem_limit_bytes=28 * 1024 * 1024),
        name="arrange",
    )(incoming)


def solution(mesh):
    placed = (
        P("ctx", "rows"),
        P("ctx", None),
        P("ctx", None),
        P("rows", None),
        P("rows", None),
        P("ctx"),
    )
    return jax.shard_map(
        body, mesh=mesh, in_specs=placed, out_specs=P(("ctx", "rows"), None), check_vma=False
    )
```

```python
import functools

import jax
import jax.numpy as jnp
from jax import lax
from jax.experimental import pallas as pl
from jax.experimental.pallas import tpu as pltpu
from jax.sharding import PartitionSpec as P

HEADS = 32
KV_HEADS = 8
DH = 128
BLOCK = 128
NEG = -1e30
ROW_CEILING = 1 << 30
EMPTY = 1048576.0
SCALE2 = DH**-0.5 * 1.4426950408889634
GROUP = 4
SLOT = 32
PIECE = {(0, 0): 0, (3, 0): 1, (1, 0): 2, (0, 1): 3, (2, 0): 4, (1, 1): 5, (3, 1): 6, (2, 1): 7}
ANY = pl.BlockSpec(memory_space=pl.ANY)
SMEM = pl.BlockSpec(memory_space=pltpu.SMEM)
VMEM = pl.BlockSpec(memory_space=pltpu.VMEM)


def dot_t(a, b):
    return lax.dot_general(a, b, (((1,), (1,)), ((), ())), preferred_element_type=jnp.float32)


def sent_kernel(meta, keys, values, sent_ref, value_s, sem):
    column = pl.ds(pl.multiple_of(meta[1] * DH, DH), DH)

    @pl.when(meta[0] == 0)
    def _():
        pltpu.make_async_copy(keys.at[:, column], value_s, sem.at[0]).start()

    @pl.when(meta[0] != 0)
    def _():
        pltpu.make_async_copy(values.at[:, column], value_s, sem.at[0]).start()

    pltpu.make_async_copy(keys.at[:, column], value_s, sem.at[0]).wait()
    for start in range(0, value_s.shape[0], BLOCK):
        rows = slice(start, start + BLOCK)
        block = value_s[rows, :]
        sent_ref[rows, :] = jnp.where(meta[0] == 0, block, block.T)


def own_kernel(meta, keys, values, keys_ref, values_ref, value_s, sem):
    column = pl.ds(pl.multiple_of(meta[1] * DH, DH), DH)
    copies = [
        pltpu.make_async_copy(values.at[:, column], value_s, sem.at[0]),
        pltpu.make_async_copy(keys.at[:, column], keys_ref, sem.at[1]),
    ]
    for copy in copies:
        copy.start()
    for copy in copies:
        copy.wait()
    for start in range(0, value_s.shape[0], BLOCK):
        rows = slice(start, start + BLOCK)
        values_ref[rows, :] = value_s[rows, :].T


def attend_kernel(sizes, slots, heads, meta, lists, counts, sent, start, q_ref, rank_ref, *rest):
    rest = list(rest)
    take = lambda n: [rest.pop(0) for _ in range(n)]
    pieces = len(sizes)
    own, mine, other = take(2), take(pieces), take(pieces)
    out_ref, k_s, v_s = take(3)
    score_s = [take(heads), take(heads)]
    peak_s = [take(heads), take(heads)]
    att, sorted_s, sem = take(3)
    shard = q_ref.shape[0]
    nblk = shard // BLOCK
    core = meta[0]
    key_copies, value_copies = [], []
    for number, (ref, to, held) in enumerate(zip(own, (k_s, v_s), (key_copies, value_copies))):
        copy = pltpu.make_async_copy(ref, to.at[pl.ds(0, shard)], sem.at[number])
        copy.start()
        held.append(copy)
    begin = shard
    for p in range(pieces):
        spot = pl.ds(begin, sizes[p])
        begin += sizes[p]
        number = 2 + 2 * p

        @pl.when(core == 0)
        def _():
            pltpu.make_async_copy(mine[p], k_s.at[spot], sem.at[number]).start()
            pltpu.make_async_copy(other[p], v_s.at[spot], sem.at[number + 1]).start()

        @pl.when(core != 0)
        def _():
            pltpu.make_async_copy(other[p], k_s.at[spot], sem.at[number]).start()
            pltpu.make_async_copy(mine[p], v_s.at[spot], sem.at[number + 1]).start()

        key_copies.append(pltpu.make_async_copy(mine[p], k_s.at[spot], sem.at[number]))
        value_copies.append(pltpu.make_async_copy(mine[p], v_s.at[spot], sem.at[number + 1]))

    def block_of(ref, index):
        return ref[pl.ds(pl.multiple_of(index * BLOCK, BLOCK), BLOCK), :]

    def lane_of(h):
        return slice(h * DH, (h + 1) * DH)

    chunks = [[-1]] + [list(range(c, min(c + GROUP, slots))) for c in range(0, slots, GROUP)]

    def place(slot):
        return slice((slot + 1) * BLOCK, (slot + 2) * BLOCK)

    def fold(reduced, block):
        return reduced(block.reshape(-1, 8, BLOCK), axis=0)

    def score(qb, h, turn, group, peaks):
        row = h * nblk + qb
        query = block_of(q_ref, qb)[:, lane_of(h)]
        if group == [-1]:
            tri = lax.broadcasted_iota(jnp.int32, (BLOCK, BLOCK), 0) <= lax.broadcasted_iota(
                jnp.int32, (BLOCK, BLOCK), 1
            )
            parts = [jnp.where(tri, dot_t(block_of(k_s, qb), query), NEG)]
        else:
            keys_block = jnp.concatenate([block_of(k_s, lists[row, u]) for u in group], axis=0)
            scores = dot_t(keys_block, query)
            parts = [scores[i * BLOCK : (i + 1) * BLOCK] for i in range(len(group))]
        for u, one in zip(group, parts):
            score_s[turn][h][place(u), :] = one
            peak = jnp.where(u < counts[row], fold(jnp.max, one), NEG)
            peaks[h] = jnp.maximum(peaks[h], peak) if h in peaks else peak
        if group == chunks[-1]:
            peak_s[turn][h][...] = peaks[h]

    def mix(qb, h, turn, group, state):
        high, total, mixed = state
        row = h * nblk + qb
        tops = [jnp.where(u < counts[row], high, -NEG) for u in group]
        weights = [jnp.exp2((score_s[turn][h][place(u), :] - top) * SCALE2) for u, top in zip(group, tops)]
        low = jnp.concatenate([w.astype(jnp.bfloat16) for w in weights], axis=0)
        values_block = jnp.concatenate([block_of(v_s, qb if u < 0 else lists[row, u]) for u in group], axis=1)
        fresh = jnp.dot(values_block, low, preferred_element_type=jnp.float32)
        for w in weights:
            total = fold(jnp.sum, w) if total is None else total + fold(jnp.sum, w)
        return high, total, fresh if mixed is None else mixed + fresh

    def phase(qb, turn, ahead):
        if qb is not None:
            states = [(jnp.max(peak_s[turn][h][...], axis=0, keepdims=True), None, None) for h in range(heads)]
        peaks = {}
        for group in chunks:
            for h in range(heads):
                score(ahead, h, 1 - turn, group, peaks)
            if qb is not None:
                for h in range(heads):
                    states[h] = mix(qb, h, turn, group, states[h])
        if qb is not None:
            for h in range(heads):
                _, total, mixed = states[h]
                attended = mixed / jnp.sum(total, axis=0, keepdims=True)
                rows = pl.ds(pl.multiple_of((qb * heads + h) * DH, DH), DH)
                att[rows, :] = attended.astype(jnp.bfloat16)

    for copy in key_copies:
        copy.wait()

    def lead(qb, _):
        phase(None, 1, qb)
        return 0

    lax.fori_loop(0, jnp.minimum(counts[0], 0) + 1, lead, 0)
    for copy in value_copies:
        copy.wait()

    def two_blocks(pair, _):
        qb = 2 * pair
        phase(qb, 0, qb + 1)
        phase(qb + 1, 1, jnp.minimum(qb + 2, nblk - 1))
        return 0

    lax.fori_loop(0, nblk // 2, two_blocks, 0)
    scatter_rows(sent, start, rank_ref, att, sorted_s, out_ref)


def scatter_rows(sent, start, rank_ref, att, sorted_s, out_ref):
    shard = rank_ref.shape[1]
    nblk = shard // BLOCK
    width = att.shape[0] // nblk
    owners = sent.shape[0]
    batch = 512

    def per_batch(step, _):
        place = lax.broadcasted_iota(jnp.int32, (batch, shard), 0)
        hot = jnp.where(rank_ref[...] - step * batch == place, 1.0, 0.0).astype(jnp.bfloat16)
        rows = pl.ds(pl.multiple_of(step * batch, batch), batch)
        sorted_s[rows, :] = dot_t(hot, jnp.concatenate([att[i * width : (i + 1) * width, :] for i in range(nblk)], axis=1))
        return 0

    lax.fori_loop(0, shard // batch, per_batch, 0)
    sorted_s[shard:, :] = jnp.zeros((SLOT + 8, width), jnp.float32)

    def per_owners(step, _):
        line = lax.broadcasted_iota(jnp.int32, (SLOT, width), 0)
        for u in range(8):
            owner = step * 8 + u
            shift = lax.rem(start[owner], 8)
            rows = sorted_s[pl.ds(pl.multiple_of(start[owner] - shift, 8), SLOT + 8), :]
            rows = pltpu.roll(rows, SLOT + 8 - shift, 0)[:SLOT]
            kept = jnp.where(line < sent[owner], rows, EMPTY).astype(jnp.bfloat16)
            out_ref[pl.ds(pl.multiple_of(owner * SLOT, SLOT), SLOT), :] = kept
        return 0

    lax.fori_loop(0, owners // 8, per_owners, 0)


def arrange_kernel(in_ref, out_ref):
    shards, groups, capacity, width = in_ref.shape
    slots = shards * capacity
    rows = out_ref.shape[0]
    block = in_ref[:, 0].reshape(slots, width)
    used = jnp.where(block[:, :rows].astype(jnp.float32) < EMPTY / 2, 1.0, 0.0).astype(jnp.bfloat16)
    one = lax.broadcasted_iota(jnp.int32, (slots, slots), 0)
    two = lax.broadcasted_iota(jnp.int32, (slots, slots), 1)
    contract = (((0,), (0,)), ((), ()))
    before = lax.dot_general(
        used, jnp.where(one < two, 1.0, 0.0).astype(jnp.bfloat16), contract, preferred_element_type=jnp.float32
    )
    here = lax.dot_general(
        used, jnp.where(one == two, 1.0, 0.0).astype(jnp.bfloat16), contract, preferred_element_type=jnp.float32
    )
    line = lax.broadcasted_iota(jnp.int32, (rows, slots), 0).astype(jnp.float32)
    pick = jnp.where((before == line) & (here > 0.5), 1.0, 0.0).astype(jnp.bfloat16)
    for g in range(groups):
        block = in_ref[:, g].reshape(slots, width)
        out_ref[:, g * width : (g + 1) * width] = jnp.dot(pick, block, preferred_element_type=jnp.float32).astype(
            jnp.bfloat16
        )


def block_lists(verticals, slashes, place, nblk, nshards):
    heads = verticals.shape[0]
    query_blocks = place * nblk + jnp.arange(nblk, dtype=jnp.int32)
    vertical = jnp.broadcast_to(verticals[:, None, :], (heads, nblk, verticals.shape[1]))
    slash = query_blocks[None, :, None] - slashes[:, None, :]
    cand = jnp.concatenate([vertical, slash], axis=2)
    slots = cand.shape[2]
    order = jnp.arange(slots, dtype=jnp.int32)
    earlier = order[None, :] < order[:, None]
    repeated = jnp.any((cand[:, :, :, None] == cand[:, :, None, :]) & earlier[None, None], axis=3)
    valid = (cand >= 0) & (cand < query_blocks[None, :, None]) & jnp.logical_not(repeated)
    source = cand // nblk
    dx = (source // 2 - place // 2) % (nshards // 2)
    dz = (source - place) % 2
    piece = jnp.zeros_like(cand)
    for (ox, oz), number in PIECE.items():
        piece = jnp.where((dx == ox) & (dz == oz), number, piece)
    local = jnp.clip(piece * nblk + cand % nblk, 0, nshards * nblk - 1)
    rank = jnp.sum((valid[:, :, None, :] & earlier[None, None]).astype(jnp.int32), axis=3)
    chosen = valid[:, :, :, None] & (rank[:, :, :, None] == order)
    lists = jnp.sum(jnp.where(chosen, local[:, :, :, None], 0), axis=2)
    return lists.reshape(heads * nblk, slots), jnp.sum(valid.astype(jnp.int32), axis=2).reshape(heads * nblk)


def body(queries, keys, values, verticals, slashes, destination):
    cycle = lax.axis_size("ctx")
    groups = lax.axis_size("rows")
    place = lax.axis_index("ctx")
    rows_here = queries.shape[0]
    heads = verticals.shape[0]
    nblk = rows_here // BLOCK
    devices = cycle * groups
    own_rows = rows_here // groups
    group = lax.axis_index("rows")
    meta = jnp.stack([group % 2, group * heads // (HEADS // KV_HEADS)]).astype(jnp.int32)
    piece = jax.ShapeDtypeStruct((rows_here, DH), jnp.bfloat16)

    def slices(kernel, outs, keys, values):
        return pl.pallas_call(
            kernel,
            out_shape=[piece] * outs,
            in_specs=[SMEM, ANY, ANY],
            out_specs=[VMEM] * outs,
            scratch_shapes=[pltpu.VMEM((rows_here, DH), jnp.bfloat16), pltpu.SemaphoreType.DMA((outs,))],
            compiler_params=pltpu.CompilerParams(vmem_limit_bytes=60 * 1024 * 1024),
            name="own",
        )(meta, keys, values)

    (own,) = slices(sent_kernel, 1, keys, values)

    def along_x(x, step):
        return lax.ppermute(x, "ctx", [(c, (c + 2 * step) % cycle) for c in range(cycle)])

    def along_z(x):
        return lax.ppermute(x, "ctx", [(c, c ^ 1) for c in range(cycle)])

    def swap(x):
        return lax.ppermute(x, "rows", [(r, r ^ 1) for r in range(groups)])

    half = rows_here // 2
    owner = destination // own_rows
    member = owner[:, None] == jnp.arange(devices, dtype=jnp.int32)[None, :]
    first_row = jnp.min(jnp.where(member, destination[:, None], ROW_CEILING), axis=0)
    sent = jnp.sum(member.astype(jnp.int32), axis=0)
    numbers = jnp.arange(devices, dtype=jnp.int32)
    start = jnp.sum(jnp.where(numbers[:, None] < numbers[None, :], sent[:, None], 0), axis=0)
    rank = destination + jnp.sum(jnp.where(member, (start - first_row)[None, :], 0), axis=1)
    p1 = along_x(own, 1)
    p3 = along_z(own)
    own, sent, keys, values = lax.optimization_barrier((own, sent, keys, values))
    p2 = along_x(own, -1)
    here = slices(own_kernel, 2, keys, values)
    lists, counts = block_lists(verticals, slashes, place, nblk, cycle)
    small = (lists, counts, sent, start, rank.reshape(1, rows_here))
    p1, p3, small, here = lax.optimization_barrier((p1, p3, small, here))

    p4 = along_x(p1, 1)
    p5 = along_x(p3, -1)
    p6 = along_z(p1)
    mine = [jnp.concatenate([p1, p2, p3], axis=0)]
    other = [swap(mine[0])]
    p7 = along_x(p6[:half], 1)
    p8 = along_x(p5[half:], -1)
    mine += [jnp.concatenate([p4, p5, p6], axis=0), p7, p8]
    other += [swap(x) for x in mine[1:]]

    lists, counts, sent, start, rank = small
    slots = lists.shape[1]
    outgoing = pl.pallas_call(
        functools.partial(attend_kernel, [x.shape[0] for x in mine], slots, heads),
        out_shape=jax.ShapeDtypeStruct((devices * SLOT, heads * DH), jnp.bfloat16),
        in_specs=[SMEM] * 5 + [VMEM] * 2 + [ANY] * (2 + 2 * len(mine)),
        out_specs=VMEM,
        scratch_shapes=[pltpu.VMEM((cycle * rows_here, DH), jnp.bfloat16)] * 2
        + [pltpu.VMEM(((slots + 1) * BLOCK, BLOCK), jnp.float32)] * (2 * heads)
        + [pltpu.VMEM((8, BLOCK), jnp.float32)] * (2 * heads)
        + [
            pltpu.VMEM((nblk * heads * DH, BLOCK), jnp.bfloat16),
            pltpu.VMEM((rows_here + SLOT + 8, heads * DH), jnp.float32),
            pltpu.SemaphoreType.DMA((2 + 2 * len(mine),)),
        ],
        compiler_params=pltpu.CompilerParams(vmem_limit_bytes=28 * 1024 * 1024),
        name="attend",
    )(meta, lists, counts, sent, start, queries, rank, *here, *mine, *other)

    incoming = lax.all_to_all(
        outgoing.reshape(devices, SLOT, heads * DH), ("ctx", "rows"), split_axis=0, concat_axis=0, tiled=True
    )
    incoming = incoming.reshape(cycle, groups, SLOT, heads * DH)
    return pl.pallas_call(
        arrange_kernel,
        out_shape=jax.ShapeDtypeStruct((own_rows, groups * heads * DH), jnp.bfloat16),
        in_specs=[VMEM],
        out_specs=VMEM,
        compiler_params=pltpu.CompilerParams(vmem_limit_bytes=28 * 1024 * 1024),
        name="arrange",
    )(incoming)


def solution(mesh):
    placed = (
        P("ctx", "rows"),
        P("ctx", None),
        P("ctx", None),
        P("rows", None),
        P("rows", None),
        P("ctx"),
    )
    return jax.shard_map(
        body, mesh=mesh, in_specs=placed, out_specs=P(("ctx", "rows"), None), check_vma=False
    )
```

```python
import functools

import jax
import jax.numpy as jnp
from jax import lax
from jax.experimental import pallas as pl
from jax.experimental.pallas import tpu as pltpu
from jax.sharding import PartitionSpec as P

HEADS = 32
KV_HEADS = 8
DH = 128
BLOCK = 128
NEG = -1e30
ROW_CEILING = 1 << 30
EMPTY = 1048576.0
SCALE2 = DH**-0.5 * 1.4426950408889634
GROUP = 4
SLOT = 32
PIECE = {(0, 0): 0, (3, 0): 1, (1, 0): 2, (0, 1): 3, (2, 0): 4, (1, 1): 5, (3, 1): 6, (2, 1): 7}
ANY = pl.BlockSpec(memory_space=pl.ANY)
SMEM = pl.BlockSpec(memory_space=pltpu.SMEM)
VMEM = pl.BlockSpec(memory_space=pltpu.VMEM)


def dot_t(a, b):
    return lax.dot_general(a, b, (((1,), (1,)), ((), ())), preferred_element_type=jnp.float32)


def own_kernel(keys, values, own_ref, keys_ref, values_ref, value_s, sem):
    core = lax.rem(lax.axis_index("rows"), 2)
    head = lax.axis_index("rows") * (HEADS // lax.axis_size("rows")) // (HEADS // KV_HEADS)
    column = pl.ds(pl.multiple_of(head * DH, DH), DH)
    parts = [slice(start, start + BLOCK) for start in range(0, value_s.shape[0], BLOCK)]
    copies = []
    for i, rows in enumerate(parts):
        copies.append(
            (
                pltpu.make_async_copy(values.at[rows, column], value_s.at[rows], sem.at[2 * i]),
                pltpu.make_async_copy(keys.at[rows, column], keys_ref.at[rows], sem.at[2 * i + 1]),
            )
        )
    for value_copy, key_copy in copies:
        value_copy.start()
        key_copy.start()
    for rows, (value_copy, key_copy) in zip(parts, copies):
        value_copy.wait()
        turned = value_s[rows, :].T
        values_ref[rows, :] = turned
        key_copy.wait()
        own_ref[rows, :] = jnp.where(core == 0, keys_ref[rows, :], turned)


def attend_kernel(sizes, slots, heads, lists, counts, sent, start, q_ref, rank_ref, *rest):
    rest = list(rest)
    take = lambda n: [rest.pop(0) for _ in range(n)]
    pieces = len(sizes)
    own, mine, other = take(2), take(pieces), take(pieces)
    out_ref, k_s, v_s = take(3)
    score_s = [take(heads), take(heads)]
    peak_s = [take(heads), take(heads)]
    att, sorted_s, sem = take(3)
    shard = q_ref.shape[0]
    nblk = shard // BLOCK
    core = lax.rem(lax.axis_index("rows"), 2)
    key_copies, value_copies = [], []
    for number, (ref, to, held) in enumerate(zip(own, (k_s, v_s), (key_copies, value_copies))):
        copy = pltpu.make_async_copy(ref, to.at[pl.ds(0, shard)], sem.at[number])
        copy.start()
        held.append(copy)
    begin = shard
    for p in range(pieces):
        spot = pl.ds(begin, sizes[p])
        begin += sizes[p]
        number = 2 + 2 * p

        @pl.when(core == 0)
        def _():
            pltpu.make_async_copy(mine[p], k_s.at[spot], sem.at[number]).start()
            pltpu.make_async_copy(other[p], v_s.at[spot], sem.at[number + 1]).start()

        @pl.when(core != 0)
        def _():
            pltpu.make_async_copy(other[p], k_s.at[spot], sem.at[number]).start()
            pltpu.make_async_copy(mine[p], v_s.at[spot], sem.at[number + 1]).start()

        key_copies.append(pltpu.make_async_copy(mine[p], k_s.at[spot], sem.at[number]))
        value_copies.append(pltpu.make_async_copy(mine[p], v_s.at[spot], sem.at[number + 1]))

    def block_of(ref, index):
        return ref[pl.ds(pl.multiple_of(index * BLOCK, BLOCK), BLOCK), :]

    def lane_of(h):
        return slice(h * DH, (h + 1) * DH)

    chunks = [[-1]] + [list(range(c, min(c + GROUP, slots))) for c in range(0, slots, GROUP)]

    def place(slot):
        return slice((slot + 1) * BLOCK, (slot + 2) * BLOCK)

    def fold(reduced, block):
        return reduced(block.reshape(-1, 8, BLOCK), axis=0)

    def score(qb, h, turn, group, peaks):
        row = h * nblk + qb
        query = block_of(q_ref, qb)[:, lane_of(h)]
        if group == [-1]:
            tri = lax.broadcasted_iota(jnp.int32, (BLOCK, BLOCK), 0) <= lax.broadcasted_iota(
                jnp.int32, (BLOCK, BLOCK), 1
            )
            parts = [jnp.where(tri, dot_t(block_of(k_s, qb), query), NEG)]
        else:
            keys_block = jnp.concatenate([block_of(k_s, lists[row, u]) for u in group], axis=0)
            scores = dot_t(keys_block, query)
            parts = [scores[i * BLOCK : (i + 1) * BLOCK] for i in range(len(group))]
        for u, one in zip(group, parts):
            score_s[turn][h][place(u), :] = one
            peak = jnp.where(u < counts[row], fold(jnp.max, one), NEG)
            peaks[h] = jnp.maximum(peaks[h], peak) if h in peaks else peak
        if group == chunks[-1]:
            peak_s[turn][h][...] = peaks[h]

    def mix(qb, h, turn, group, state):
        high, total, mixed = state
        row = h * nblk + qb
        tops = [jnp.where(u < counts[row], high, -NEG) for u in group]
        weights = [jnp.exp2((score_s[turn][h][place(u), :] - top) * SCALE2) for u, top in zip(group, tops)]
        low = jnp.concatenate([w.astype(jnp.bfloat16) for w in weights], axis=0)
        values_block = jnp.concatenate([block_of(v_s, qb if u < 0 else lists[row, u]) for u in group], axis=1)
        fresh = jnp.dot(values_block, low, preferred_element_type=jnp.float32)
        for w in weights:
            total = fold(jnp.sum, w) if total is None else total + fold(jnp.sum, w)
        return high, total, fresh if mixed is None else mixed + fresh

    def phase(qb, turn, ahead):
        if qb is not None:
            states = [(jnp.max(peak_s[turn][h][...], axis=0, keepdims=True), None, None) for h in range(heads)]
        peaks = {}
        for group in chunks:
            for h in range(heads):
                score(ahead, h, 1 - turn, group, peaks)
            if qb is not None:
                for h in range(heads):
                    states[h] = mix(qb, h, turn, group, states[h])
        if qb is not None:
            for h in range(heads):
                _, total, mixed = states[h]
                attended = mixed / jnp.sum(total, axis=0, keepdims=True)
                rows = pl.ds(pl.multiple_of((qb * heads + h) * DH, DH), DH)
                att[rows, :] = attended.astype(jnp.bfloat16)

    for copy in key_copies:
        copy.wait()

    def lead(qb, _):
        phase(None, 1, qb)
        return 0

    lax.fori_loop(0, jnp.minimum(counts[0], 0) + 1, lead, 0)
    for copy in value_copies:
        copy.wait()

    def two_blocks(pair, _):
        qb = 2 * pair
        phase(qb, 0, qb + 1)
        phase(qb + 1, 1, jnp.minimum(qb + 2, nblk - 1))
        return 0

    lax.fori_loop(0, nblk // 2, two_blocks, 0)
    scatter_rows(sent, start, rank_ref, att, sorted_s, out_ref)


def scatter_rows(sent, start, rank_ref, att, sorted_s, out_ref):
    shard = rank_ref.shape[1]
    nblk = shard // BLOCK
    width = att.shape[0] // nblk
    owners = sent.shape[0]
    batch = 512

    def per_batch(step, _):
        place = lax.broadcasted_iota(jnp.int32, (batch, shard), 0)
        hot = jnp.where(rank_ref[...] - step * batch == place, 1.0, 0.0).astype(jnp.bfloat16)
        rows = pl.ds(pl.multiple_of(step * batch, batch), batch)
        sorted_s[rows, :] = dot_t(hot, jnp.concatenate([att[i * width : (i + 1) * width, :] for i in range(nblk)], axis=1))
        return 0

    lax.fori_loop(0, shard // batch, per_batch, 0)
    sorted_s[shard:, :] = jnp.zeros((SLOT + 8, width), jnp.float32)

    def per_owners(step, _):
        line = lax.broadcasted_iota(jnp.int32, (SLOT, width), 0)
        for u in range(8):
            owner = step * 8 + u
            shift = lax.rem(start[owner], 8)
            rows = sorted_s[pl.ds(pl.multiple_of(start[owner] - shift, 8), SLOT + 8), :]
            rows = pltpu.roll(rows, SLOT + 8 - shift, 0)[:SLOT]
            kept = jnp.where(line < sent[owner], rows, EMPTY).astype(jnp.bfloat16)
            out_ref[pl.ds(pl.multiple_of(owner * SLOT, SLOT), SLOT), :] = kept
        return 0

    lax.fori_loop(0, owners // 8, per_owners, 0)


def arrange_kernel(in_ref, out_ref):
    shards, groups, capacity, width = in_ref.shape
    slots = shards * capacity
    rows = out_ref.shape[0]
    block = in_ref[:, 0].reshape(slots, width)
    used = jnp.where(block[:, :rows].astype(jnp.float32) < EMPTY / 2, 1.0, 0.0).astype(jnp.bfloat16)
    one = lax.broadcasted_iota(jnp.int32, (slots, slots), 0)
    two = lax.broadcasted_iota(jnp.int32, (slots, slots), 1)
    contract = (((0,), (0,)), ((), ()))
    before = lax.dot_general(
        used, jnp.where(one < two, 1.0, 0.0).astype(jnp.bfloat16), contract, preferred_element_type=jnp.float32
    )
    here = lax.dot_general(
        used, jnp.where(one == two, 1.0, 0.0).astype(jnp.bfloat16), contract, preferred_element_type=jnp.float32
    )
    line = lax.broadcasted_iota(jnp.int32, (rows, slots), 0).astype(jnp.float32)
    pick = jnp.where((before == line) & (here > 0.5), 1.0, 0.0).astype(jnp.bfloat16)
    for g in range(groups):
        block = in_ref[:, g].reshape(slots, width)
        out_ref[:, g * width : (g + 1) * width] = jnp.dot(pick, block, preferred_element_type=jnp.float32).astype(
            jnp.bfloat16
        )


def block_lists(verticals, slashes, place, nblk, nshards):
    heads = verticals.shape[0]
    query_blocks = place * nblk + jnp.arange(nblk, dtype=jnp.int32)
    vertical = jnp.broadcast_to(verticals[:, None, :], (heads, nblk, verticals.shape[1]))
    slash = query_blocks[None, :, None] - slashes[:, None, :]
    cand = jnp.concatenate([vertical, slash], axis=2)
    slots = cand.shape[2]
    order = jnp.arange(slots, dtype=jnp.int32)
    earlier = order[None, :] < order[:, None]
    repeated = jnp.any((cand[:, :, :, None] == cand[:, :, None, :]) & earlier[None, None], axis=3)
    valid = (cand >= 0) & (cand < query_blocks[None, :, None]) & jnp.logical_not(repeated)
    source = cand // nblk
    dx = (source // 2 - place // 2) % (nshards // 2)
    dz = (source - place) % 2
    piece = jnp.zeros_like(cand)
    for (ox, oz), number in PIECE.items():
        piece = jnp.where((dx == ox) & (dz == oz), number, piece)
    local = jnp.clip(piece * nblk + cand % nblk, 0, nshards * nblk - 1)
    rank = jnp.sum((valid[:, :, None, :] & earlier[None, None]).astype(jnp.int32), axis=3)
    chosen = valid[:, :, :, None] & (rank[:, :, :, None] == order)
    lists = jnp.sum(jnp.where(chosen, local[:, :, :, None], 0), axis=2)
    return lists.reshape(heads * nblk, slots), jnp.sum(valid.astype(jnp.int32), axis=2).reshape(heads * nblk)


def body(queries, keys, values, verticals, slashes, destination):
    cycle = lax.axis_size("ctx")
    groups = lax.axis_size("rows")
    place = lax.axis_index("ctx")
    rows_here = queries.shape[0]
    heads = verticals.shape[0]
    nblk = rows_here // BLOCK
    devices = cycle * groups
    own_rows = rows_here // groups
    own, *here = pl.pallas_call(
        own_kernel,
        out_shape=[jax.ShapeDtypeStruct((rows_here, DH), jnp.bfloat16)] * 3,
        in_specs=[ANY, ANY],
        out_specs=[VMEM] * 3,
        scratch_shapes=[pltpu.VMEM((rows_here, DH), jnp.bfloat16), pltpu.SemaphoreType.DMA((2 * nblk,))],
        compiler_params=pltpu.CompilerParams(vmem_limit_bytes=60 * 1024 * 1024),
        name="own",
    )(keys, values)

    def along_x(x, step):
        return lax.ppermute(x, "ctx", [(c, (c + 2 * step) % cycle) for c in range(cycle)])

    def along_z(x):
        return lax.ppermute(x, "ctx", [(c, c ^ 1) for c in range(cycle)])

    def swap(x):
        return lax.ppermute(x, "rows", [(r, r ^ 1) for r in range(groups)])

    half = rows_here // 2
    owner = destination // own_rows
    member = owner[:, None] == jnp.arange(devices, dtype=jnp.int32)[None, :]
    first_row = jnp.min(jnp.where(member, destination[:, None], ROW_CEILING), axis=0)
    sent = jnp.sum(member.astype(jnp.int32), axis=0)
    numbers = jnp.arange(devices, dtype=jnp.int32)
    start = jnp.sum(jnp.where(numbers[:, None] < numbers[None, :], sent[:, None], 0), axis=0)
    rank = destination + jnp.sum(jnp.where(member, (start - first_row)[None, :], 0), axis=1)
    p1 = along_x(own, 1)
    p3 = along_z(own)
    own, sent = lax.optimization_barrier((own, sent))
    p2 = along_x(own, -1)
    lists, counts = block_lists(verticals, slashes, place, nblk, cycle)
    small = (lists, counts, sent, start, rank.reshape(1, rows_here))
    p1, small = lax.optimization_barrier((p1, small))

    p4 = along_x(p1, 1)
    p5 = along_x(p3, -1)
    p6 = along_z(p1)
    mine = [jnp.concatenate([p1, p2, p3], axis=0)]
    other = [swap(mine[0])]
    p7 = along_x(p6[:half], 1)
    p8 = along_x(p5[half:], -1)
    mine += [jnp.concatenate([p4, p5, p6], axis=0), p7, p8]
    other += [swap(x) for x in mine[1:]]

    lists, counts, sent, start, rank = small
    slots = lists.shape[1]
    outgoing = pl.pallas_call(
        functools.partial(attend_kernel, [x.shape[0] for x in mine], slots, heads),
        out_shape=jax.ShapeDtypeStruct((devices * SLOT, heads * DH), jnp.bfloat16),
        in_specs=[SMEM] * 4 + [VMEM] * 2 + [ANY] * (2 + 2 * len(mine)),
        out_specs=VMEM,
        scratch_shapes=[pltpu.VMEM((cycle * rows_here, DH), jnp.bfloat16)] * 2
        + [pltpu.VMEM(((slots + 1) * BLOCK, BLOCK), jnp.float32)] * (2 * heads)
        + [pltpu.VMEM((8, BLOCK), jnp.float32)] * (2 * heads)
        + [
            pltpu.VMEM((nblk * heads * DH, BLOCK), jnp.bfloat16),
            pltpu.VMEM((rows_here + SLOT + 8, heads * DH), jnp.float32),
            pltpu.SemaphoreType.DMA((2 + 2 * len(mine),)),
        ],
        compiler_params=pltpu.CompilerParams(vmem_limit_bytes=28 * 1024 * 1024),
        name="attend",
    )(lists, counts, sent, start, queries, rank, *here, *mine, *other)

    incoming = lax.all_to_all(
        outgoing.reshape(devices, SLOT, heads * DH), ("ctx", "rows"), split_axis=0, concat_axis=0, tiled=True
    )
    incoming = incoming.reshape(cycle, groups, SLOT, heads * DH)
    return pl.pallas_call(
        arrange_kernel,
        out_shape=jax.ShapeDtypeStruct((own_rows, groups * heads * DH), jnp.bfloat16),
        in_specs=[VMEM],
        out_specs=VMEM,
        compiler_params=pltpu.CompilerParams(vmem_limit_bytes=28 * 1024 * 1024),
        name="arrange",
    )(incoming)


def solution(mesh):
    placed = (
        P("ctx", "rows"),
        P("ctx", None),
        P("ctx", None),
        P("rows", None),
        P("rows", None),
        P("ctx"),
    )
    return jax.shard_map(
        body, mesh=mesh, in_specs=placed, out_specs=P(("ctx", "rows"), None), check_vma=False
    )
```

```python
import functools

import jax
import jax.numpy as jnp
from jax import lax
from jax.experimental import pallas as pl
from jax.experimental.pallas import tpu as pltpu
from jax.sharding import PartitionSpec as P

HEADS = 32
KV_HEADS = 8
DH = 128
BLOCK = 128
NEG = -1e30
ROW_CEILING = 1 << 30
EMPTY = 1048576.0
SCALE2 = DH**-0.5 * 1.4426950408889634
GROUP = 4
SLOT = 32
PIECE = {(0, 0): 0, (3, 0): 1, (1, 0): 2, (0, 1): 3, (2, 0): 4, (1, 1): 5, (3, 1): 6, (2, 1): 7}
ANY = pl.BlockSpec(memory_space=pl.ANY)
SMEM = pl.BlockSpec(memory_space=pltpu.SMEM)
VMEM = pl.BlockSpec(memory_space=pltpu.VMEM)


def dot_t(a, b):
    return lax.dot_general(a, b, (((1,), (1,)), ((), ())), preferred_element_type=jnp.float32)


def turn_kernel(block_ref, out_ref):
    core = lax.rem(lax.axis_index("rows"), 2)
    for start in range(0, block_ref.shape[0], BLOCK):
        rows = slice(start, start + BLOCK)
        block = block_ref[rows, :]
        out_ref[rows, :] = jnp.where(core == 0, block, block.T)


def own_kernel(keys, values, keys_ref, values_ref, value_s, sem):
    head = lax.axis_index("rows") * (HEADS // lax.axis_size("rows")) // (HEADS // KV_HEADS)
    column = pl.ds(pl.multiple_of(head * DH, DH), DH)
    copies = [
        pltpu.make_async_copy(values.at[:, column], value_s, sem.at[0]),
        pltpu.make_async_copy(keys.at[:, column], keys_ref, sem.at[1]),
    ]
    for copy in copies:
        copy.start()
    for copy in copies:
        copy.wait()
    for start in range(0, value_s.shape[0], BLOCK):
        rows = slice(start, start + BLOCK)
        values_ref[rows, :] = value_s[rows, :].T


def attend_kernel(sizes, slots, heads, lists, counts, sent, start, q_ref, rank_ref, *rest):
    rest = list(rest)
    take = lambda n: [rest.pop(0) for _ in range(n)]
    pieces = len(sizes)
    own, mine, other = take(2), take(pieces), take(pieces)
    out_ref, k_s, v_s = take(3)
    score_s = [take(heads), take(heads)]
    peak_s = [take(heads), take(heads)]
    att, sorted_s, sem = take(3)
    shard = q_ref.shape[0]
    nblk = shard // BLOCK
    core = lax.rem(lax.axis_index("rows"), 2)
    key_copies, value_copies = [], []
    for number, (ref, to, held) in enumerate(zip(own, (k_s, v_s), (key_copies, value_copies))):
        copy = pltpu.make_async_copy(ref, to.at[pl.ds(0, shard)], sem.at[number])
        copy.start()
        held.append(copy)
    begin = shard
    for p in range(pieces):
        spot = pl.ds(begin, sizes[p])
        begin += sizes[p]
        number = 2 + 2 * p

        @pl.when(core == 0)
        def _():
            pltpu.make_async_copy(mine[p], k_s.at[spot], sem.at[number]).start()
            pltpu.make_async_copy(other[p], v_s.at[spot], sem.at[number + 1]).start()

        @pl.when(core != 0)
        def _():
            pltpu.make_async_copy(other[p], k_s.at[spot], sem.at[number]).start()
            pltpu.make_async_copy(mine[p], v_s.at[spot], sem.at[number + 1]).start()

        key_copies.append(pltpu.make_async_copy(mine[p], k_s.at[spot], sem.at[number]))
        value_copies.append(pltpu.make_async_copy(mine[p], v_s.at[spot], sem.at[number + 1]))

    def block_of(ref, index):
        return ref[pl.ds(pl.multiple_of(index * BLOCK, BLOCK), BLOCK), :]

    def lane_of(h):
        return slice(h * DH, (h + 1) * DH)

    chunks = [[-1]] + [list(range(c, min(c + GROUP, slots))) for c in range(0, slots, GROUP)]

    def place(slot):
        return slice((slot + 1) * BLOCK, (slot + 2) * BLOCK)

    def fold(reduced, block):
        return reduced(block.reshape(-1, 8, BLOCK), axis=0)

    def score(qb, h, turn, group, peaks):
        row = h * nblk + qb
        query = block_of(q_ref, qb)[:, lane_of(h)]
        if group == [-1]:
            tri = lax.broadcasted_iota(jnp.int32, (BLOCK, BLOCK), 0) <= lax.broadcasted_iota(
                jnp.int32, (BLOCK, BLOCK), 1
            )
            parts = [jnp.where(tri, dot_t(block_of(k_s, qb), query), NEG)]
        else:
            keys_block = jnp.concatenate([block_of(k_s, lists[row, u]) for u in group], axis=0)
            scores = dot_t(keys_block, query)
            parts = [scores[i * BLOCK : (i + 1) * BLOCK] for i in range(len(group))]
        for u, one in zip(group, parts):
            score_s[turn][h][place(u), :] = one
            peak = jnp.where(u < counts[row], fold(jnp.max, one), NEG)
            peaks[h] = jnp.maximum(peaks[h], peak) if h in peaks else peak
        if group == chunks[-1]:
            peak_s[turn][h][...] = peaks[h]

    def mix(qb, h, turn, group, state):
        high, total, mixed = state
        row = h * nblk + qb
        tops = [jnp.where(u < counts[row], high, -NEG) for u in group]
        weights = [jnp.exp2((score_s[turn][h][place(u), :] - top) * SCALE2) for u, top in zip(group, tops)]
        low = jnp.concatenate([w.astype(jnp.bfloat16) for w in weights], axis=0)
        values_block = jnp.concatenate([block_of(v_s, qb if u < 0 else lists[row, u]) for u in group], axis=1)
        fresh = jnp.dot(values_block, low, preferred_element_type=jnp.float32)
        for w in weights:
            total = fold(jnp.sum, w) if total is None else total + fold(jnp.sum, w)
        return high, total, fresh if mixed is None else mixed + fresh

    def phase(qb, turn, ahead):
        if qb is not None:
            states = [(jnp.max(peak_s[turn][h][...], axis=0, keepdims=True), None, None) for h in range(heads)]
        peaks = {}
        for group in chunks:
            for h in range(heads):
                score(ahead, h, 1 - turn, group, peaks)
            if qb is not None:
                for h in range(heads):
                    states[h] = mix(qb, h, turn, group, states[h])
        if qb is not None:
            for h in range(heads):
                _, total, mixed = states[h]
                attended = mixed / jnp.sum(total, axis=0, keepdims=True)
                rows = pl.ds(pl.multiple_of((qb * heads + h) * DH, DH), DH)
                att[rows, :] = attended.astype(jnp.bfloat16)

    for copy in key_copies:
        copy.wait()

    def lead(qb, _):
        phase(None, 1, qb)
        return 0

    lax.fori_loop(0, jnp.minimum(counts[0], 0) + 1, lead, 0)
    for copy in value_copies:
        copy.wait()

    def two_blocks(pair, _):
        qb = 2 * pair
        phase(qb, 0, qb + 1)
        phase(qb + 1, 1, jnp.minimum(qb + 2, nblk - 1))
        return 0

    lax.fori_loop(0, nblk // 2, two_blocks, 0)
    scatter_rows(sent, start, rank_ref, att, sorted_s, out_ref)


def scatter_rows(sent, start, rank_ref, att, sorted_s, out_ref):
    shard = rank_ref.shape[1]
    nblk = shard // BLOCK
    width = att.shape[0] // nblk
    owners = sent.shape[0]
    batch = 512

    def per_batch(step, _):
        place = lax.broadcasted_iota(jnp.int32, (batch, shard), 0)
        hot = jnp.where(rank_ref[...] - step * batch == place, 1.0, 0.0).astype(jnp.bfloat16)
        rows = pl.ds(pl.multiple_of(step * batch, batch), batch)
        sorted_s[rows, :] = dot_t(hot, jnp.concatenate([att[i * width : (i + 1) * width, :] for i in range(nblk)], axis=1))
        return 0

    lax.fori_loop(0, shard // batch, per_batch, 0)
    sorted_s[shard:, :] = jnp.zeros((SLOT + 8, width), jnp.float32)

    def per_owners(step, _):
        line = lax.broadcasted_iota(jnp.int32, (SLOT, width), 0)
        for u in range(8):
            owner = step * 8 + u
            shift = lax.rem(start[owner], 8)
            rows = sorted_s[pl.ds(pl.multiple_of(start[owner] - shift, 8), SLOT + 8), :]
            rows = pltpu.roll(rows, SLOT + 8 - shift, 0)[:SLOT]
            kept = jnp.where(line < sent[owner], rows, EMPTY).astype(jnp.bfloat16)
            out_ref[pl.ds(pl.multiple_of(owner * SLOT, SLOT), SLOT), :] = kept
        return 0

    lax.fori_loop(0, owners // 8, per_owners, 0)


def arrange_kernel(in_ref, out_ref):
    shards, groups, capacity, width = in_ref.shape
    slots = shards * capacity
    rows = out_ref.shape[0]
    block = in_ref[:, 0].reshape(slots, width)
    used = jnp.where(block[:, :rows].astype(jnp.float32) < EMPTY / 2, 1.0, 0.0).astype(jnp.bfloat16)
    one = lax.broadcasted_iota(jnp.int32, (slots, slots), 0)
    two = lax.broadcasted_iota(jnp.int32, (slots, slots), 1)
    contract = (((0,), (0,)), ((), ()))
    before = lax.dot_general(
        used, jnp.where(one < two, 1.0, 0.0).astype(jnp.bfloat16), contract, preferred_element_type=jnp.float32
    )
    here = lax.dot_general(
        used, jnp.where(one == two, 1.0, 0.0).astype(jnp.bfloat16), contract, preferred_element_type=jnp.float32
    )
    line = lax.broadcasted_iota(jnp.int32, (rows, slots), 0).astype(jnp.float32)
    pick = jnp.where((before == line) & (here > 0.5), 1.0, 0.0).astype(jnp.bfloat16)
    for g in range(groups):
        block = in_ref[:, g].reshape(slots, width)
        out_ref[:, g * width : (g + 1) * width] = jnp.dot(pick, block, preferred_element_type=jnp.float32).astype(
            jnp.bfloat16
        )


def block_lists(verticals, slashes, place, nblk, nshards):
    heads = verticals.shape[0]
    query_blocks = place * nblk + jnp.arange(nblk, dtype=jnp.int32)
    vertical = jnp.broadcast_to(verticals[:, None, :], (heads, nblk, verticals.shape[1]))
    slash = query_blocks[None, :, None] - slashes[:, None, :]
    cand = jnp.concatenate([vertical, slash], axis=2)
    slots = cand.shape[2]
    order = jnp.arange(slots, dtype=jnp.int32)
    earlier = order[None, :] < order[:, None]
    repeated = jnp.any((cand[:, :, :, None] == cand[:, :, None, :]) & earlier[None, None], axis=3)
    valid = (cand >= 0) & (cand < query_blocks[None, :, None]) & jnp.logical_not(repeated)
    source = cand // nblk
    dx = (source // 2 - place // 2) % (nshards // 2)
    dz = (source - place) % 2
    piece = jnp.zeros_like(cand)
    for (ox, oz), number in PIECE.items():
        piece = jnp.where((dx == ox) & (dz == oz), number, piece)
    local = jnp.clip(piece * nblk + cand % nblk, 0, nshards * nblk - 1)
    rank = jnp.sum((valid[:, :, None, :] & earlier[None, None]).astype(jnp.int32), axis=3)
    chosen = valid[:, :, :, None] & (rank[:, :, :, None] == order)
    lists = jnp.sum(jnp.where(chosen, local[:, :, :, None], 0), axis=2)
    return lists.reshape(heads * nblk, slots), jnp.sum(valid.astype(jnp.int32), axis=2).reshape(heads * nblk)


def body(queries, keys, values, verticals, slashes, destination):
    cycle = lax.axis_size("ctx")
    groups = lax.axis_size("rows")
    place = lax.axis_index("ctx")
    rows_here = queries.shape[0]
    heads = verticals.shape[0]
    nblk = rows_here // BLOCK
    devices = cycle * groups
    own_rows = rows_here // groups
    group = lax.axis_index("rows")
    head = group * heads // (HEADS // KV_HEADS)
    piece = jax.ShapeDtypeStruct((rows_here, DH), jnp.bfloat16)
    own = pl.pallas_call(
        turn_kernel,
        out_shape=piece,
        in_specs=[VMEM],
        out_specs=VMEM,
        compiler_params=pltpu.CompilerParams(vmem_limit_bytes=24 * 1024 * 1024),
        name="turn",
    )(
        jnp.where(
            group % 2 == 0,
            lax.dynamic_slice_in_dim(keys, head * DH, DH, 1),
            lax.dynamic_slice_in_dim(values, head * DH, DH, 1),
        )
    )

    def along_x(x, step):
        return lax.ppermute(x, "ctx", [(c, (c + 2 * step) % cycle) for c in range(cycle)])

    def along_z(x):
        return lax.ppermute(x, "ctx", [(c, c ^ 1) for c in range(cycle)])

    def swap(x):
        return lax.ppermute(x, "rows", [(r, r ^ 1) for r in range(groups)])

    cut = rows_here * 5 // 8
    owner = destination // own_rows
    member = owner[:, None] == jnp.arange(devices, dtype=jnp.int32)[None, :]
    first_row = jnp.min(jnp.where(member, destination[:, None], ROW_CEILING), axis=0)
    sent = jnp.sum(member.astype(jnp.int32), axis=0)
    numbers = jnp.arange(devices, dtype=jnp.int32)
    start = jnp.sum(jnp.where(numbers[:, None] < numbers[None, :], sent[:, None], 0), axis=0)
    rank = destination + jnp.sum(jnp.where(member, (start - first_row)[None, :], 0), axis=1)
    p1 = along_x(own, 1)
    p3 = along_z(own)
    own, sent, keys, values = lax.optimization_barrier((own, sent, keys, values))
    p2 = along_x(own, -1)
    here = pl.pallas_call(
        own_kernel,
        out_shape=[piece] * 2,
        in_specs=[ANY, ANY],
        out_specs=[VMEM] * 2,
        scratch_shapes=[pltpu.VMEM((rows_here, DH), jnp.bfloat16), pltpu.SemaphoreType.DMA((2,))],
        compiler_params=pltpu.CompilerParams(vmem_limit_bytes=60 * 1024 * 1024),
        name="own",
    )(keys, values)
    lists, counts = block_lists(verticals, slashes, place, nblk, cycle)
    small = (lists, counts, sent, start, rank.reshape(1, rows_here))
    p1, small, here = lax.optimization_barrier((p1, small, here))

    p4 = along_x(p1, 1)
    p5 = along_x(p3, -1)
    p6 = along_z(p1)
    mine = [jnp.concatenate([p1, p2, p3], axis=0)]
    other = [swap(mine[0])]
    p7 = along_x(p6[:cut], 1)
    p8 = along_x(p5[cut:], -1)
    mine += [jnp.concatenate([p4, p5, p6], axis=0), p7, p8]
    other += [swap(x) for x in mine[1:]]

    lists, counts, sent, start, rank = small
    slots = lists.shape[1]
    outgoing = pl.pallas_call(
        functools.partial(attend_kernel, [x.shape[0] for x in mine], slots, heads),
        out_shape=jax.ShapeDtypeStruct((devices * SLOT, heads * DH), jnp.bfloat16),
        in_specs=[SMEM] * 4 + [VMEM] * 2 + [ANY] * (2 + 2 * len(mine)),
        out_specs=VMEM,
        scratch_shapes=[pltpu.VMEM((cycle * rows_here, DH), jnp.bfloat16)] * 2
        + [pltpu.VMEM(((slots + 1) * BLOCK, BLOCK), jnp.float32)] * (2 * heads)
        + [pltpu.VMEM((8, BLOCK), jnp.float32)] * (2 * heads)
        + [
            pltpu.VMEM((nblk * heads * DH, BLOCK), jnp.bfloat16),
            pltpu.VMEM((rows_here + SLOT + 8, heads * DH), jnp.float32),
            pltpu.SemaphoreType.DMA((2 + 2 * len(mine),)),
        ],
        compiler_params=pltpu.CompilerParams(vmem_limit_bytes=28 * 1024 * 1024),
        name="attend",
    )(lists, counts, sent, start, queries, rank, *here, *mine, *other)

    incoming = lax.all_to_all(
        outgoing.reshape(devices, SLOT, heads * DH), ("ctx", "rows"), split_axis=0, concat_axis=0, tiled=True
    )
    incoming = incoming.reshape(cycle, groups, SLOT, heads * DH)
    return pl.pallas_call(
        arrange_kernel,
        out_shape=jax.ShapeDtypeStruct((own_rows, groups * heads * DH), jnp.bfloat16),
        in_specs=[VMEM],
        out_specs=VMEM,
        compiler_params=pltpu.CompilerParams(vmem_limit_bytes=28 * 1024 * 1024),
        name="arrange",
    )(incoming)


def solution(mesh):
    placed = (
        P("ctx", "rows"),
        P("ctx", None),
        P("ctx", None),
        P("rows", None),
        P("rows", None),
        P("ctx"),
    )
    return jax.shard_map(
        body, mesh=mesh, in_specs=placed, out_specs=P(("ctx", "rows"), None), check_vma=False
    )
```

```python
import functools

import jax
import jax.numpy as jnp
from jax import lax
from jax.experimental import pallas as pl
from jax.experimental.pallas import tpu as pltpu
from jax.sharding import PartitionSpec as P

HEADS = 32
KV_HEADS = 8
DH = 128
BLOCK = 128
NEG = -1e30
ROW_CEILING = 1 << 30
EMPTY = 1048576.0
SCALE2 = DH**-0.5 * 1.4426950408889634
GROUP = 4
SLOT = 32
PIECE = {(0, 0): 0, (3, 0): 1, (1, 0): 2, (0, 1): 3, (2, 0): 4, (1, 1): 5, (3, 1): 6, (2, 1): 7}
ANY = pl.BlockSpec(memory_space=pl.ANY)
SMEM = pl.BlockSpec(memory_space=pltpu.SMEM)
VMEM = pl.BlockSpec(memory_space=pltpu.VMEM)


def dot_t(a, b):
    return lax.dot_general(a, b, (((1,), (1,)), ((), ())), preferred_element_type=jnp.float32)


def turn_kernel(block_ref, out_ref):
    core = lax.rem(lax.axis_index("rows"), 2)
    for start in range(0, block_ref.shape[0], BLOCK):
        rows = slice(start, start + BLOCK)
        block = block_ref[rows, :]
        out_ref[rows, :] = jnp.where(core == 0, block, block.T)


def own_kernel(keys, values, keys_ref, values_ref, value_s, sem):
    head = lax.axis_index("rows") * (HEADS // lax.axis_size("rows")) // (HEADS // KV_HEADS)
    column = pl.ds(pl.multiple_of(head * DH, DH), DH)
    copies = [
        pltpu.make_async_copy(values.at[:, column], value_s, sem.at[0]),
        pltpu.make_async_copy(keys.at[:, column], keys_ref, sem.at[1]),
    ]
    for copy in copies:
        copy.start()
    for copy in copies:
        copy.wait()
    for start in range(0, value_s.shape[0], BLOCK):
        rows = slice(start, start + BLOCK)
        values_ref[rows, :] = value_s[rows, :].T


def attend_kernel(sizes, slots, heads, lists, counts, sent, start, q_ref, rank_ref, *rest):
    rest = list(rest)
    take = lambda n: [rest.pop(0) for _ in range(n)]
    pieces = len(sizes)
    own, mine, other = take(2), take(pieces), take(pieces)
    out_ref, k_s, v_s = take(3)
    score_s = [take(heads), take(heads)]
    peak_s = [take(heads), take(heads)]
    att, sorted_s, sem = take(3)
    shard = q_ref.shape[0]
    nblk = shard // BLOCK
    core = lax.rem(lax.axis_index("rows"), 2)
    key_copies, value_copies = [], []
    for number, (ref, to, held) in enumerate(zip(own, (k_s, v_s), (key_copies, value_copies))):
        copy = pltpu.make_async_copy(ref, to.at[pl.ds(0, shard)], sem.at[number])
        copy.start()
        held.append(copy)
    begin = shard
    for p in range(pieces):
        spot = pl.ds(begin, sizes[p])
        begin += sizes[p]
        number = 2 + 2 * p

        @pl.when(core == 0)
        def _():
            pltpu.make_async_copy(mine[p], k_s.at[spot], sem.at[number]).start()
            pltpu.make_async_copy(other[p], v_s.at[spot], sem.at[number + 1]).start()

        @pl.when(core != 0)
        def _():
            pltpu.make_async_copy(other[p], k_s.at[spot], sem.at[number]).start()
            pltpu.make_async_copy(mine[p], v_s.at[spot], sem.at[number + 1]).start()

        key_copies.append(pltpu.make_async_copy(mine[p], k_s.at[spot], sem.at[number]))
        value_copies.append(pltpu.make_async_copy(mine[p], v_s.at[spot], sem.at[number + 1]))

    def block_of(ref, index):
        return ref[pl.ds(pl.multiple_of(index * BLOCK, BLOCK), BLOCK), :]

    def lane_of(h):
        return slice(h * DH, (h + 1) * DH)

    chunks = [[-1]] + [list(range(c, min(c + GROUP, slots))) for c in range(0, slots, GROUP)]

    def place(slot):
        return slice((slot + 1) * BLOCK, (slot + 2) * BLOCK)

    def fold(reduced, block):
        return reduced(block.reshape(-1, 8, BLOCK), axis=0)

    def score(qb, h, turn, group, peaks):
        row = h * nblk + qb
        query = block_of(q_ref, qb)[:, lane_of(h)]
        if group == [-1]:
            tri = lax.broadcasted_iota(jnp.int32, (BLOCK, BLOCK), 0) <= lax.broadcasted_iota(
                jnp.int32, (BLOCK, BLOCK), 1
            )
            parts = [jnp.where(tri, dot_t(block_of(k_s, qb), query), NEG)]
        else:
            keys_block = jnp.concatenate([block_of(k_s, lists[row, u]) for u in group], axis=0)
            scores = dot_t(keys_block, query)
            parts = [scores[i * BLOCK : (i + 1) * BLOCK] for i in range(len(group))]
        for u, one in zip(group, parts):
            score_s[turn][h][place(u), :] = one
            peak = jnp.where(u < counts[row], fold(jnp.max, one), NEG)
            peaks[h] = jnp.maximum(peaks[h], peak) if h in peaks else peak
        if group == chunks[-1]:
            peak_s[turn][h][...] = peaks[h]

    def mix(qb, h, turn, group, state):
        high, total, mixed = state
        row = h * nblk + qb
        tops = [jnp.where(u < counts[row], high, -NEG) for u in group]
        weights = [jnp.exp2((score_s[turn][h][place(u), :] - top) * SCALE2) for u, top in zip(group, tops)]
        low = jnp.concatenate([w.astype(jnp.bfloat16) for w in weights], axis=0)
        values_block = jnp.concatenate([block_of(v_s, qb if u < 0 else lists[row, u]) for u in group], axis=1)
        fresh = jnp.dot(values_block, low, preferred_element_type=jnp.float32)
        for w in weights:
            total = fold(jnp.sum, w) if total is None else total + fold(jnp.sum, w)
        return high, total, fresh if mixed is None else mixed + fresh

    def phase(qb, turn, ahead):
        if qb is not None:
            states = [(jnp.max(peak_s[turn][h][...], axis=0, keepdims=True), None, None) for h in range(heads)]
        peaks = {}
        for group in chunks:
            for h in range(heads):
                score(ahead, h, 1 - turn, group, peaks)
            if qb is not None:
                for h in range(heads):
                    states[h] = mix(qb, h, turn, group, states[h])
        if qb is not None:
            for h in range(heads):
                _, total, mixed = states[h]
                attended = mixed / jnp.sum(total, axis=0, keepdims=True)
                rows = pl.ds(pl.multiple_of((qb * heads + h) * DH, DH), DH)
                att[rows, :] = attended.astype(jnp.bfloat16)

    for copy in key_copies:
        copy.wait()

    def lead(qb, _):
        phase(None, 1, qb)
        return 0

    lax.fori_loop(0, jnp.minimum(counts[0], 0) + 1, lead, 0)
    for copy in value_copies:
        copy.wait()

    def two_blocks(pair, _):
        qb = 2 * pair
        phase(qb, 0, qb + 1)
        phase(qb + 1, 1, jnp.minimum(qb + 2, nblk - 1))
        return 0

    lax.fori_loop(0, nblk // 2, two_blocks, 0)
    scatter_rows(sent, start, rank_ref, att, sorted_s, out_ref)


def scatter_rows(sent, start, rank_ref, att, sorted_s, out_ref):
    shard = rank_ref.shape[1]
    nblk = shard // BLOCK
    width = att.shape[0] // nblk
    owners = sent.shape[0]
    batch = 512

    def per_batch(step, _):
        place = lax.broadcasted_iota(jnp.int32, (batch, shard), 0)
        hot = jnp.where(rank_ref[...] - step * batch == place, 1.0, 0.0).astype(jnp.bfloat16)
        rows = pl.ds(pl.multiple_of(step * batch, batch), batch)
        sorted_s[rows, :] = dot_t(hot, jnp.concatenate([att[i * width : (i + 1) * width, :] for i in range(nblk)], axis=1))
        return 0

    lax.fori_loop(0, shard // batch, per_batch, 0)
    sorted_s[shard:, :] = jnp.zeros((SLOT + 8, width), jnp.float32)

    def per_owners(step, _):
        line = lax.broadcasted_iota(jnp.int32, (SLOT, width), 0)
        for u in range(8):
            owner = step * 8 + u
            shift = lax.rem(start[owner], 8)
            rows = sorted_s[pl.ds(pl.multiple_of(start[owner] - shift, 8), SLOT + 8), :]
            rows = pltpu.roll(rows, SLOT + 8 - shift, 0)[:SLOT]
            kept = jnp.where(line < sent[owner], rows, EMPTY).astype(jnp.bfloat16)
            out_ref[pl.ds(pl.multiple_of(owner * SLOT, SLOT), SLOT), :] = kept
        return 0

    lax.fori_loop(0, owners // 8, per_owners, 0)


def arrange_kernel(in_ref, out_ref):
    shards, groups, capacity, width = in_ref.shape
    slots = shards * capacity
    rows = out_ref.shape[0]
    block = in_ref[:, 0].reshape(slots, width)
    used = jnp.where(block[:, :rows].astype(jnp.float32) < EMPTY / 2, 1.0, 0.0).astype(jnp.bfloat16)
    one = lax.broadcasted_iota(jnp.int32, (slots, slots), 0)
    two = lax.broadcasted_iota(jnp.int32, (slots, slots), 1)
    contract = (((0,), (0,)), ((), ()))
    before = lax.dot_general(
        used, jnp.where(one < two, 1.0, 0.0).astype(jnp.bfloat16), contract, preferred_element_type=jnp.float32
    )
    here = lax.dot_general(
        used, jnp.where(one == two, 1.0, 0.0).astype(jnp.bfloat16), contract, preferred_element_type=jnp.float32
    )
    line = lax.broadcasted_iota(jnp.int32, (rows, slots), 0).astype(jnp.float32)
    pick = jnp.where((before == line) & (here > 0.5), 1.0, 0.0).astype(jnp.bfloat16)
    for g in range(groups):
        block = in_ref[:, g].reshape(slots, width)
        out_ref[:, g * width : (g + 1) * width] = jnp.dot(pick, block, preferred_element_type=jnp.float32).astype(
            jnp.bfloat16
        )


def block_lists(verticals, slashes, place, nblk, nshards):
    heads = verticals.shape[0]
    query_blocks = place * nblk + jnp.arange(nblk, dtype=jnp.int32)
    vertical = jnp.broadcast_to(verticals[:, None, :], (heads, nblk, verticals.shape[1]))
    slash = query_blocks[None, :, None] - slashes[:, None, :]
    cand = jnp.concatenate([vertical, slash], axis=2)
    slots = cand.shape[2]
    order = jnp.arange(slots, dtype=jnp.int32)
    earlier = order[None, :] < order[:, None]
    repeated = jnp.any((cand[:, :, :, None] == cand[:, :, None, :]) & earlier[None, None], axis=3)
    valid = (cand >= 0) & (cand < query_blocks[None, :, None]) & jnp.logical_not(repeated)
    source = cand // nblk
    dx = (source // 2 - place // 2) % (nshards // 2)
    dz = (source - place) % 2
    piece = jnp.zeros_like(cand)
    for (ox, oz), number in PIECE.items():
        piece = jnp.where((dx == ox) & (dz == oz), number, piece)
    local = jnp.clip(piece * nblk + cand % nblk, 0, nshards * nblk - 1)
    rank = jnp.sum((valid[:, :, None, :] & earlier[None, None]).astype(jnp.int32), axis=3)
    chosen = valid[:, :, :, None] & (rank[:, :, :, None] == order)
    lists = jnp.sum(jnp.where(chosen, local[:, :, :, None], 0), axis=2)
    return lists.reshape(heads * nblk, slots), jnp.sum(valid.astype(jnp.int32), axis=2).reshape(heads * nblk)


def body(queries, keys, values, verticals, slashes, destination):
    cycle = lax.axis_size("ctx")
    groups = lax.axis_size("rows")
    place = lax.axis_index("ctx")
    rows_here = queries.shape[0]
    heads = verticals.shape[0]
    nblk = rows_here // BLOCK
    devices = cycle * groups
    own_rows = rows_here // groups
    group = lax.axis_index("rows")
    head = group * heads // (HEADS // KV_HEADS)
    piece = jax.ShapeDtypeStruct((rows_here, DH), jnp.bfloat16)
    own = pl.pallas_call(
        turn_kernel,
        out_shape=piece,
        in_specs=[VMEM],
        out_specs=VMEM,
        compiler_params=pltpu.CompilerParams(vmem_limit_bytes=24 * 1024 * 1024),
        name="turn",
    )(
        jnp.where(
            group % 2 == 0,
            lax.dynamic_slice_in_dim(keys, head * DH, DH, 1),
            lax.dynamic_slice_in_dim(values, head * DH, DH, 1),
        )
    )

    def along_x(x, step):
        return lax.ppermute(x, "ctx", [(c, (c + 2 * step) % cycle) for c in range(cycle)])

    def along_z(x):
        return lax.ppermute(x, "ctx", [(c, c ^ 1) for c in range(cycle)])

    def swap(x):
        return lax.ppermute(x, "rows", [(r, r ^ 1) for r in range(groups)])

    cut = rows_here // 2
    owner = destination // own_rows
    member = owner[:, None] == jnp.arange(devices, dtype=jnp.int32)[None, :]
    first_row = jnp.min(jnp.where(member, destination[:, None], ROW_CEILING), axis=0)
    sent = jnp.sum(member.astype(jnp.int32), axis=0)
    numbers = jnp.arange(devices, dtype=jnp.int32)
    start = jnp.sum(jnp.where(numbers[:, None] < numbers[None, :], sent[:, None], 0), axis=0)
    rank = destination + jnp.sum(jnp.where(member, (start - first_row)[None, :], 0), axis=1)
    p1 = along_x(own, 1)
    p3 = along_z(own)
    own, sent, keys, values = lax.optimization_barrier((own, sent, keys, values))
    p2 = along_x(own, -1)
    here = pl.pallas_call(
        own_kernel,
        out_shape=[piece] * 2,
        in_specs=[ANY, ANY],
        out_specs=[VMEM] * 2,
        scratch_shapes=[pltpu.VMEM((rows_here, DH), jnp.bfloat16), pltpu.SemaphoreType.DMA((2,))],
        compiler_params=pltpu.CompilerParams(vmem_limit_bytes=60 * 1024 * 1024),
        name="own",
    )(keys, values)
    lists, counts = block_lists(verticals, slashes, place, nblk, cycle)
    small = (lists, counts, sent, start, rank.reshape(1, rows_here))
    p1, small, here = lax.optimization_barrier((p1, small, here))

    p4 = along_x(p1, 1)
    p5 = along_x(p3, -1)
    p6 = along_z(p1)
    mine = [jnp.concatenate([p1, p2, p3], axis=0)]
    other = [swap(mine[0])]
    p7 = along_x(p6[:cut], 1)
    p8 = along_x(p5[cut:], -1)
    mine += [jnp.concatenate([p4, p5, p6], axis=0), p7, p8]
    other += [swap(x) for x in mine[1:]]

    lists, counts, sent, start, rank = small
    slots = lists.shape[1]
    outgoing = pl.pallas_call(
        functools.partial(attend_kernel, [x.shape[0] for x in mine], slots, heads),
        out_shape=jax.ShapeDtypeStruct((devices * SLOT, heads * DH), jnp.bfloat16),
        in_specs=[SMEM] * 4 + [VMEM] * 2 + [ANY] * (2 + 2 * len(mine)),
        out_specs=VMEM,
        scratch_shapes=[pltpu.VMEM((cycle * rows_here, DH), jnp.bfloat16)] * 2
        + [pltpu.VMEM(((slots + 1) * BLOCK, BLOCK), jnp.float32)] * (2 * heads)
        + [pltpu.VMEM((8, BLOCK), jnp.float32)] * (2 * heads)
        + [
            pltpu.VMEM((nblk * heads * DH, BLOCK), jnp.bfloat16),
            pltpu.VMEM((rows_here + SLOT + 8, heads * DH), jnp.float32),
            pltpu.SemaphoreType.DMA((2 + 2 * len(mine),)),
        ],
        compiler_params=pltpu.CompilerParams(vmem_limit_bytes=32 * 1024 * 1024),
        name="attend",
    )(lists, counts, sent, start, queries, rank, *here, *mine, *other)

    incoming = lax.all_to_all(
        outgoing.reshape(devices, SLOT, heads * DH), ("ctx", "rows"), split_axis=0, concat_axis=0, tiled=True
    )
    incoming = incoming.reshape(cycle, groups, SLOT, heads * DH)
    return pl.pallas_call(
        arrange_kernel,
        out_shape=jax.ShapeDtypeStruct((own_rows, groups * heads * DH), jnp.bfloat16),
        in_specs=[VMEM],
        out_specs=VMEM,
        compiler_params=pltpu.CompilerParams(vmem_limit_bytes=28 * 1024 * 1024),
        name="arrange",
    )(incoming)


def solution(mesh):
    placed = (
        P("ctx", "rows"),
        P("ctx", None),
        P("ctx", None),
        P("rows", None),
        P("rows", None),
        P("ctx"),
    )
    return jax.shard_map(
        body, mesh=mesh, in_specs=placed, out_specs=P(("ctx", "rows"), None), check_vma=False
    )
```

```python
import functools

import jax
import jax.numpy as jnp
from jax import lax
from jax.experimental import pallas as pl
from jax.experimental.pallas import tpu as pltpu
from jax.sharding import PartitionSpec as P

HEADS = 32
KV_HEADS = 8
DH = 128
BLOCK = 128
NEG = -1e30
ROW_CEILING = 1 << 30
EMPTY = 1048576.0
SCALE2 = DH**-0.5 * 1.4426950408889634
GROUP = 4
SLOT = 32
PIECE = {(0, 0): 0, (3, 0): 1, (1, 0): 2, (0, 1): 3, (2, 0): 4, (1, 1): 5, (3, 1): 6, (2, 1): 7}
ANY = pl.BlockSpec(memory_space=pl.ANY)
SMEM = pl.BlockSpec(memory_space=pltpu.SMEM)
VMEM = pl.BlockSpec(memory_space=pltpu.VMEM)


def dot_t(a, b):
    return lax.dot_general(a, b, (((1,), (1,)), ((), ())), preferred_element_type=jnp.float32)


def turn_kernel(block_ref, out_ref):
    core = lax.rem(lax.axis_index("rows"), 2)
    for start in range(0, block_ref.shape[0], BLOCK):
        rows = slice(start, start + BLOCK)
        block = block_ref[rows, :]
        out_ref[rows, :] = jnp.where(core == 0, block, block.T)


def own_kernel(keys, values, keys_ref, values_ref, value_s, sem):
    head = lax.axis_index("rows") * (HEADS // lax.axis_size("rows")) // (HEADS // KV_HEADS)
    column = pl.ds(pl.multiple_of(head * DH, DH), DH)
    copies = [
        pltpu.make_async_copy(values.at[:, column], value_s, sem.at[0]),
        pltpu.make_async_copy(keys.at[:, column], keys_ref, sem.at[1]),
    ]
    for copy in copies:
        copy.start()
    for copy in copies:
        copy.wait()
    for start in range(0, value_s.shape[0], BLOCK):
        rows = slice(start, start + BLOCK)
        values_ref[rows, :] = value_s[rows, :].T


def attend_kernel(sizes, slots, heads, lists, counts, sent, start, q_ref, rank_ref, *rest):
    rest = list(rest)
    take = lambda n: [rest.pop(0) for _ in range(n)]
    pieces = len(sizes)
    own, mine, other = take(2), take(pieces), take(pieces)
    out_ref, k_s, v_s = take(3)
    score_s = [take(heads), take(heads)]
    peak_s = [take(heads), take(heads)]
    att, sorted_s, sem = take(3)
    shard = q_ref.shape[0]
    nblk = shard // BLOCK
    core = lax.rem(lax.axis_index("rows"), 2)
    key_copies, value_copies = [], []
    for number, (ref, to, held) in enumerate(zip(own, (k_s, v_s), (key_copies, value_copies))):
        copy = pltpu.make_async_copy(ref, to.at[pl.ds(0, shard)], sem.at[number])
        copy.start()
        held.append(copy)
    begin = shard
    for p in range(pieces):
        spot = pl.ds(begin, sizes[p])
        begin += sizes[p]
        number = 2 + 2 * p

        @pl.when(core == 0)
        def _():
            pltpu.make_async_copy(mine[p], k_s.at[spot], sem.at[number]).start()
            pltpu.make_async_copy(other[p], v_s.at[spot], sem.at[number + 1]).start()

        @pl.when(core != 0)
        def _():
            pltpu.make_async_copy(other[p], k_s.at[spot], sem.at[number]).start()
            pltpu.make_async_copy(mine[p], v_s.at[spot], sem.at[number + 1]).start()

        key_copies.append(pltpu.make_async_copy(mine[p], k_s.at[spot], sem.at[number]))
        value_copies.append(pltpu.make_async_copy(mine[p], v_s.at[spot], sem.at[number + 1]))

    def block_of(ref, index):
        return ref[pl.ds(pl.multiple_of(index * BLOCK, BLOCK), BLOCK), :]

    def lane_of(h):
        return slice(h * DH, (h + 1) * DH)

    chunks = [[-1]] + [list(range(c, min(c + GROUP, slots))) for c in range(0, slots, GROUP)]

    def place(slot):
        return slice((slot + 1) * BLOCK, (slot + 2) * BLOCK)

    def fold(reduced, block):
        return reduced(block.reshape(-1, 8, BLOCK), axis=0)

    def score(qb, h, turn, group, peaks):
        row = h * nblk + qb
        query = block_of(q_ref, qb)[:, lane_of(h)]
        if group == [-1]:
            tri = lax.broadcasted_iota(jnp.int32, (BLOCK, BLOCK), 0) <= lax.broadcasted_iota(
                jnp.int32, (BLOCK, BLOCK), 1
            )
            parts = [jnp.where(tri, dot_t(block_of(k_s, qb), query), NEG)]
        else:
            keys_block = jnp.concatenate([block_of(k_s, lists[row, u]) for u in group], axis=0)
            scores = dot_t(keys_block, query)
            parts = [scores[i * BLOCK : (i + 1) * BLOCK] for i in range(len(group))]
        for u, one in zip(group, parts):
            score_s[turn][h][place(u), :] = one
            peak = jnp.where(u < counts[row], fold(jnp.max, one), NEG)
            peaks[h] = jnp.maximum(peaks[h], peak) if h in peaks else peak
        if group == chunks[-1]:
            peak_s[turn][h][...] = peaks[h]

    def mix(qb, h, turn, group, state):
        high, total, mixed = state
        row = h * nblk + qb
        tops = [jnp.where(u < counts[row], high, -NEG) for u in group]
        weights = [jnp.exp2((score_s[turn][h][place(u), :] - top) * SCALE2) for u, top in zip(group, tops)]
        low = jnp.concatenate([w.astype(jnp.bfloat16) for w in weights], axis=0)
        values_block = jnp.concatenate([block_of(v_s, qb if u < 0 else lists[row, u]) for u in group], axis=1)
        fresh = jnp.dot(values_block, low, preferred_element_type=jnp.float32)
        for w in weights:
            total = fold(jnp.sum, w) if total is None else total + fold(jnp.sum, w)
        return high, total, fresh if mixed is None else mixed + fresh

    def phase(qb, turn, ahead):
        if qb is not None:
            states = [(jnp.max(peak_s[turn][h][...], axis=0, keepdims=True), None, None) for h in range(heads)]
        peaks = {}
        for group in chunks:
            for h in range(heads):
                score(ahead, h, 1 - turn, group, peaks)
            if qb is not None:
                for h in range(heads):
                    states[h] = mix(qb, h, turn, group, states[h])
        if qb is not None:
            for h in range(heads):
                _, total, mixed = states[h]
                attended = mixed / jnp.sum(total, axis=0, keepdims=True)
                rows = pl.ds(pl.multiple_of((qb * heads + h) * DH, DH), DH)
                att[rows, :] = attended.astype(jnp.bfloat16)

    for copy in key_copies:
        copy.wait()

    def lead(qb, _):
        phase(None, 1, qb)
        return 0

    lax.fori_loop(0, jnp.minimum(counts[0], 0) + 1, lead, 0)
    for copy in value_copies:
        copy.wait()

    def two_blocks(pair, _):
        qb = 2 * pair
        phase(qb, 0, qb + 1)
        phase(qb + 1, 1, jnp.minimum(qb + 2, nblk - 1))
        return 0

    lax.fori_loop(0, nblk // 2, two_blocks, 0)
    scatter_rows(sent, start, rank_ref, att, sorted_s, out_ref)


def scatter_rows(sent, start, rank_ref, att, sorted_s, out_ref):
    shard = rank_ref.shape[1]
    nblk = shard // BLOCK
    width = att.shape[0] // nblk
    owners = sent.shape[0]
    batch = 512

    def per_batch(step, _):
        place = lax.broadcasted_iota(jnp.int32, (batch, shard), 0)
        hot = jnp.where(rank_ref[...] - step * batch == place, 1.0, 0.0).astype(jnp.bfloat16)
        rows = pl.ds(pl.multiple_of(step * batch, batch), batch)
        sorted_s[rows, :] = dot_t(hot, jnp.concatenate([att[i * width : (i + 1) * width, :] for i in range(nblk)], axis=1))
        return 0

    lax.fori_loop(0, shard // batch, per_batch, 0)
    sorted_s[shard:, :] = jnp.zeros((SLOT + 8, width), jnp.float32)

    def per_owners(step, _):
        line = lax.broadcasted_iota(jnp.int32, (SLOT, width), 0)
        for u in range(8):
            owner = step * 8 + u
            shift = lax.rem(start[owner], 8)
            rows = sorted_s[pl.ds(pl.multiple_of(start[owner] - shift, 8), SLOT + 8), :]
            rows = pltpu.roll(rows, SLOT + 8 - shift, 0)[:SLOT]
            kept = jnp.where(line < sent[owner], rows, EMPTY).astype(jnp.bfloat16)
            out_ref[pl.ds(pl.multiple_of(owner * SLOT, SLOT), SLOT), :] = kept
        return 0

    lax.fori_loop(0, owners // 8, per_owners, 0)


def arrange_kernel(in_ref, out_ref):
    shards, groups, capacity, width = in_ref.shape
    slots = shards * capacity
    rows = out_ref.shape[0]
    block = in_ref[:, 0].reshape(slots, width)
    used = jnp.where(block[:, :rows].astype(jnp.float32) < EMPTY / 2, 1.0, 0.0).astype(jnp.bfloat16)
    one = lax.broadcasted_iota(jnp.int32, (slots, slots), 0)
    two = lax.broadcasted_iota(jnp.int32, (slots, slots), 1)
    contract = (((0,), (0,)), ((), ()))
    before = lax.dot_general(
        used, jnp.where(one < two, 1.0, 0.0).astype(jnp.bfloat16), contract, preferred_element_type=jnp.float32
    )
    here = lax.dot_general(
        used, jnp.where(one == two, 1.0, 0.0).astype(jnp.bfloat16), contract, preferred_element_type=jnp.float32
    )
    line = lax.broadcasted_iota(jnp.int32, (rows, slots), 0).astype(jnp.float32)
    pick = jnp.where((before == line) & (here > 0.5), 1.0, 0.0).astype(jnp.bfloat16)
    for g in range(groups):
        block = in_ref[:, g].reshape(slots, width)
        out_ref[:, g * width : (g + 1) * width] = jnp.dot(pick, block, preferred_element_type=jnp.float32).astype(
            jnp.bfloat16
        )


def block_lists(verticals, slashes, place, nblk, nshards):
    heads = verticals.shape[0]
    query_blocks = place * nblk + jnp.arange(nblk, dtype=jnp.int32)
    vertical = jnp.broadcast_to(verticals[:, None, :], (heads, nblk, verticals.shape[1]))
    slash = query_blocks[None, :, None] - slashes[:, None, :]
    cand = jnp.concatenate([vertical, slash], axis=2)
    slots = cand.shape[2]
    order = jnp.arange(slots, dtype=jnp.int32)
    earlier = order[None, :] < order[:, None]
    repeated = jnp.any((cand[:, :, :, None] == cand[:, :, None, :]) & earlier[None, None], axis=3)
    valid = (cand >= 0) & (cand < query_blocks[None, :, None]) & jnp.logical_not(repeated)
    source = cand // nblk
    dx = (source // 2 - place // 2) % (nshards // 2)
    dz = (source - place) % 2
    piece = jnp.zeros_like(cand)
    for (ox, oz), number in PIECE.items():
        piece = jnp.where((dx == ox) & (dz == oz), number, piece)
    local = jnp.clip(piece * nblk + cand % nblk, 0, nshards * nblk - 1)
    rank = jnp.sum((valid[:, :, None, :] & earlier[None, None]).astype(jnp.int32), axis=3)
    chosen = valid[:, :, :, None] & (rank[:, :, :, None] == order)
    lists = jnp.sum(jnp.where(chosen, local[:, :, :, None], 0), axis=2)
    return lists.reshape(heads * nblk, slots), jnp.sum(valid.astype(jnp.int32), axis=2).reshape(heads * nblk)


def body(queries, keys, values, verticals, slashes, destination):
    cycle = lax.axis_size("ctx")
    groups = lax.axis_size("rows")
    place = lax.axis_index("ctx")
    rows_here = queries.shape[0]
    heads = verticals.shape[0]
    nblk = rows_here // BLOCK
    devices = cycle * groups
    own_rows = rows_here // groups
    group = lax.axis_index("rows")
    head = group * heads // (HEADS // KV_HEADS)
    piece = jax.ShapeDtypeStruct((rows_here, DH), jnp.bfloat16)
    own = pl.pallas_call(
        turn_kernel,
        out_shape=piece,
        in_specs=[VMEM],
        out_specs=VMEM,
        compiler_params=pltpu.CompilerParams(vmem_limit_bytes=24 * 1024 * 1024),
        name="turn",
    )(
        jnp.where(
            group % 2 == 0,
            lax.dynamic_slice_in_dim(keys, head * DH, DH, 1),
            lax.dynamic_slice_in_dim(values, head * DH, DH, 1),
        )
    )

    def along_x(x, step):
        return lax.ppermute(x, "ctx", [(c, (c + 2 * step) % cycle) for c in range(cycle)])

    def along_z(x):
        return lax.ppermute(x, "ctx", [(c, c ^ 1) for c in range(cycle)])

    def swap(x):
        return lax.ppermute(x, "rows", [(r, r ^ 1) for r in range(groups)])

    cut = rows_here * 9 // 16
    owner = destination // own_rows
    member = owner[:, None] == jnp.arange(devices, dtype=jnp.int32)[None, :]
    first_row = jnp.min(jnp.where(member, destination[:, None], ROW_CEILING), axis=0)
    sent = jnp.sum(member.astype(jnp.int32), axis=0)
    numbers = jnp.arange(devices, dtype=jnp.int32)
    start = jnp.sum(jnp.where(numbers[:, None] < numbers[None, :], sent[:, None], 0), axis=0)
    rank = destination + jnp.sum(jnp.where(member, (start - first_row)[None, :], 0), axis=1)
    p1 = along_x(own, 1)
    p3 = along_z(own)
    own, sent, keys, values = lax.optimization_barrier((own, sent, keys, values))
    p2 = along_x(own, -1)
    here = pl.pallas_call(
        own_kernel,
        out_shape=[piece] * 2,
        in_specs=[ANY, ANY],
        out_specs=[VMEM] * 2,
        scratch_shapes=[pltpu.VMEM((rows_here, DH), jnp.bfloat16), pltpu.SemaphoreType.DMA((2,))],
        compiler_params=pltpu.CompilerParams(vmem_limit_bytes=60 * 1024 * 1024),
        name="own",
    )(keys, values)
    lists, counts = block_lists(verticals, slashes, place, nblk, cycle)
    small = (lists, counts, sent, start, rank.reshape(1, rows_here))
    p1, small, here = lax.optimization_barrier((p1, small, here))

    p4 = along_x(p1, 1)
    p5 = along_x(p3, -1)
    p6 = along_z(p1)
    mine = [jnp.concatenate([p1, p2, p3], axis=0)]
    other = [swap(mine[0])]
    p7 = along_x(p6[:cut], 1)
    p8 = along_x(p5[cut:], -1)
    mine += [jnp.concatenate([p4, p5, p6], axis=0), p7, p8]
    other += [swap(x) for x in mine[1:]]

    lists, counts, sent, start, rank = small
    slots = lists.shape[1]
    outgoing = pl.pallas_call(
        functools.partial(attend_kernel, [x.shape[0] for x in mine], slots, heads),
        out_shape=jax.ShapeDtypeStruct((devices * SLOT, heads * DH), jnp.bfloat16),
        in_specs=[SMEM] * 4 + [VMEM] * 2 + [ANY] * (2 + 2 * len(mine)),
        out_specs=VMEM,
        scratch_shapes=[pltpu.VMEM((cycle * rows_here, DH), jnp.bfloat16)] * 2
        + [pltpu.VMEM(((slots + 1) * BLOCK, BLOCK), jnp.float32)] * (2 * heads)
        + [pltpu.VMEM((8, BLOCK), jnp.float32)] * (2 * heads)
        + [
            pltpu.VMEM((nblk * heads * DH, BLOCK), jnp.bfloat16),
            pltpu.VMEM((rows_here + SLOT + 8, heads * DH), jnp.float32),
            pltpu.SemaphoreType.DMA((2 + 2 * len(mine),)),
        ],
        compiler_params=pltpu.CompilerParams(vmem_limit_bytes=32 * 1024 * 1024),
        name="attend",
    )(lists, counts, sent, start, queries, rank, *here, *mine, *other)

    incoming = lax.all_to_all(
        outgoing.reshape(devices, SLOT, heads * DH), ("ctx", "rows"), split_axis=0, concat_axis=0, tiled=True
    )
    incoming = incoming.reshape(cycle, groups, SLOT, heads * DH)
    return pl.pallas_call(
        arrange_kernel,
        out_shape=jax.ShapeDtypeStruct((own_rows, groups * heads * DH), jnp.bfloat16),
        in_specs=[VMEM],
        out_specs=VMEM,
        compiler_params=pltpu.CompilerParams(vmem_limit_bytes=28 * 1024 * 1024),
        name="arrange",
    )(incoming)


def solution(mesh):
    placed = (
        P("ctx", "rows"),
        P("ctx", None),
        P("ctx", None),
        P("rows", None),
        P("rows", None),
        P("ctx"),
    )
    return jax.shard_map(
        body, mesh=mesh, in_specs=placed, out_specs=P(("ctx", "rows"), None), check_vma=False
    )
```
